128 devices in a mesh: dp: 16 (over x, y), expert: 8 (over z, core).
Axes of the slice: x: 4, y: 4, z: 4, core: 2. Of those that a mesh axis runs over, the one named last changes fastest.
Arguments:
- hidden: bfloat16 [16384, 2, 7168], P(('dp', 'expert')), may hold values from -6 to 6
- grad_out: bfloat16 [16384, 2048], P(('dp', 'expert')), may hold values from -6 to 6
- gate_weights: float32 [16384, 2], P(('dp', 'expert')), may hold values from 0.1 to 1
- routes: int32 [16384, 2], P(('dp', 'expert')), may hold values from 0 to 7, all different within a row; in each aligned block of 128 rows (0 to 127, 128 to 255, ...) at most 48 rows name the same one
- example_ids: int32 [16384], P(('dp', 'expert')), may hold values from 0 to 127, as said below
Outputs:
- update: bfloat16 [8, 7168, 2048], P('expert', 'dp')
- norm_ratio: float32 [128], P('dp')
The draws below stay inside these ranges and needn't reach their ends.
Inputs may be any that keep to these rules, and one draw needn't show every extreme that they name: `routes`: among the 128 tokens of one device no expert is named by more than 48 tokens, and some device reaches 48 for some expert. `example_ids`: ids never fall along the tokens; tokens i * 1024 to (i + 1) * 1024 - 1 hold exactly the examples i * 8 to (i + 1) * 8 - 1, each with one or more tokens.
All inputs are finite; a program needn't handle non-finite values.
Results may differ from the reference program's by a relative error of at most 0.019.
Values may be sent and summed in bfloat16 or wider, within the bound.
A program may use at most 128 MiB of HBM per device.

```python
import math
import jax
import jax.numpy as jnp
import numpy as np
from jax import lax

FFW = 7168
DW = 2048
TOK_DEV = 128
EX_BLK = 8
EXPERTS = 8
CAP = 48
ROWS = 384
BLOCK = 1024
TOKENS = 16384
EXAMPLES = 128
N_DP = 16
N_EXPERT = 8


def example_table(key):
    block_keys = jax.random.split(key, N_DP)

    def one_block(block_key):
        cut_points = jax.random.permutation(block_key, BLOCK - 1)[:EX_BLK - 1] + 1
        positions = jnp.arange(BLOCK, dtype=jnp.int32)
        return jnp.sum((positions[:, None] >= cut_points[None, :].astype(jnp.int32)).astype(jnp.int32), axis=1)
    local_ids = jax.vmap(one_block)(block_keys)
    offsets = jnp.arange(N_DP, dtype=jnp.int32)[:, None] * EX_BLK
    return (local_ids + offsets).reshape(-1).astype(jnp.int32)


def draw_example_ids(key, part):
    return example_table(jax.random.fold_in(key, 7))


def shared_rows(key, own_key, width, copies):
    ids = example_table(jax.random.fold_in(key, 7))
    base = jax.random.normal(jax.random.fold_in(own_key, 1), (EXAMPLES, width), jnp.float32)
    noise = jax.random.normal(jax.random.fold_in(own_key, 3), (TOKENS, copies, width), jnp.float32)
    common = base[ids]
    values = 0.6 * common[:, None, :] + 0.8 * noise
    return jnp.clip(values, -6.0, 6.0)


def draw_hidden(key, part):
    own_key = jax.random.fold_in(key, 21)
    values = shared_rows(key, own_key, FFW, 2)
    return values.astype(jnp.bfloat16)


def draw_grad_out(key, part):
    own_key = jax.random.fold_in(key, 22)
    values = shared_rows(key, own_key, DW, 1)
    return values.reshape(TOKENS, DW).astype(jnp.bfloat16)


def levels(key, shape, cuts, least, largest):
    def one(dim, shards_of):
        draws = jax.random.uniform(jax.random.fold_in(jax.random.fold_in(key, 6), dim), (shards_of,), jnp.float32, least / len(cuts), largest / len(cuts))
        return jnp.repeat(jnp.exp(draws), shape[dim] // shards_of).reshape((-1,) + (1,) * (len(shape) - dim - 1))

    loudness = one(*cuts[0])
    for cut in cuts[1:]:
        loudness = loudness * one(*cut)
    return loudness


def shared_out(stream_key, own, number, rows, number_of, top, most, lean):
    sequence = jax.random.permutation(stream_key, number_of)
    crowded, ordinary = portions_of(number_of, rows * top, most, lean, True), portions_of(number_of, rows * top, most, lean, False)
    places = jnp.arange(number_of)

    def named(sizes, rotation):
        used = int((sizes > 0).sum())
        fixed = max(1, used // 4)
        passed = fixed + (places - fixed + rotation * (used - fixed)) % max(1, number_of - fixed)
        return jnp.zeros((number_of,), jnp.int32).at[sequence[jnp.where(places < fixed, places, passed)]].set(jnp.asarray(sizes, jnp.int32))

    sizes = jnp.where(number % 4 == 0, named(crowded, number // 4), named(ordinary, number - number // 4 - 1))
    mixed = jax.random.permutation(jax.random.fold_in(own, 3), number_of)
    giver, sink = mixed[0:number_of // 2 * 2:2], mixed[1:number_of // 2 * 2:2]
    room = jnp.minimum(sizes[giver] - 1, most - sizes[sink]) // 2
    room = jnp.where((giver == sequence[0]) | (sink == sequence[0]) | (sizes[sink] == 0), 0, jnp.maximum(room, 0))
    passed = jax.random.randint(jax.random.fold_in(own, 4), (number_of // 2,), 0, 1 << 20) % (room + 1)
    sizes = sizes.at[giver].add(-passed).at[sink].add(passed)
    items = jnp.searchsorted(jnp.cumsum(sizes), jnp.arange(rows * top), side="right").astype(jnp.int32)
    listing = items.reshape(top, rows).T
    listing = listing[jax.random.permutation(jax.random.fold_in(own, 1), rows)]
    rotation = jax.random.randint(jax.random.fold_in(own, 2), (rows, 1), 0, top)
    return jnp.take_along_axis(listing, (jnp.arange(top)[None, :] + rotation) % top, axis=1)


def portions_of(amount, total, limit, lean, full):
    portions = [(1 << 20) // math.isqrt(grade ** lean) + 1 for grade in range(1, amount + 1)]
    largest = limit if full else min(limit, max(-(-total // amount), total * portions[0] // sum(portions)))
    least = 1 if total - largest >= amount - 1 else 0
    holding, rest = [largest] + [least] * (amount - 1), total - largest - least * (amount - 1)
    while rest > 0:
        candidates = [i for i in range(1, amount) if holding[i] < largest] or [i for i in range(1, amount) if holding[i] < limit]
        pool, budget = sum([portions[i] for i in candidates]), rest
        for i in candidates:
            extra = min(limit - holding[i], max(1, budget * portions[i] // pool), rest)
            holding[i] = holding[i] + extra
            rest = rest - extra
    return np.array(holding)


def setup_inputs(seed: int = 0) -> dict:
    keys = jax.random.split(jax.random.key(seed), 6)
    hidden = draw_hidden(jax.random.fold_in(keys[5], 71), 0)
    grad_out = draw_grad_out(jax.random.fold_in(keys[5], 71), 0)
    gate_weights = jnp.clip(jnp.exp(math.log(1.0) - 2.3025851 * jax.random.uniform(keys[2], (TOKENS, 2), jnp.float32) ** levels(keys[2], (TOKENS, 2), ((0, 128),), -0.2, 0.2)), 0.1, 1.0)
    routes_keys = jax.random.split(jax.random.fold_in(keys[3], 1), TOKENS // TOK_DEV)
    routes_turns = jax.random.permutation(jax.random.fold_in(keys[3], 3), TOKENS // TOK_DEV)
    routes = jax.vmap(lambda own, number: shared_out(jax.random.fold_in(keys[3], 2), own, number, TOK_DEV, EXPERTS, 2, CAP, 2))(routes_keys, routes_turns).reshape((TOKENS, 2))
    example_ids = draw_example_ids(jax.random.fold_in(keys[5], 71), 0)
    return dict(hidden=hidden, grad_out=grad_out, gate_weights=gate_weights, routes=routes, example_ids=example_ids)


def slot_targets(route_flat):
    chosen = (route_flat[:, None] == jnp.arange(EXPERTS, dtype=jnp.int32)[None, :]).astype(jnp.int32)
    position = lax.optimization_barrier(jnp.sum((jnp.cumsum(chosen, axis=0) - 1) * chosen, axis=1))
    return (route_flat * CAP + position).astype(jnp.int32)

def pack_device(hidden_dev, grads_dev, routes_dev, ids_dev):
    destin = slot_targets(routes_dev.reshape(-1).astype(jnp.int32))
    hidden_sent = jnp.zeros((EXPERTS * CAP, FFW), jnp.bfloat16).at[destin].set(hidden_dev.reshape(-1, FFW))
    grads_sent = jnp.zeros((EXPERTS * CAP, DW), jnp.bfloat16).at[destin].set(grads_dev.reshape(-1, DW))
    owner_sent = jnp.full((EXPERTS * CAP,), -1, jnp.int32).at[destin].set(jnp.repeat(ids_dev, 2).astype(jnp.int32))
    return (hidden_sent.reshape(EXPERTS, CAP, FFW), grads_sent.reshape(EXPERTS, CAP, DW), owner_sent.reshape(EXPERTS, CAP))

def gather_row(hidden_row, grads_row, routes_row, ids_row):
    packed = jax.vmap(pack_device)(hidden_row, grads_row, routes_row, ids_row)
    return tuple((jnp.swapaxes(item, 0, 1).reshape((EXPERTS, ROWS) + item.shape[3:]) for item in packed))

def belongs_to(owner_in, first_example):
    return (owner_in[:, None] == first_example + jnp.arange(EX_BLK, dtype=jnp.int32)[None, :]).astype(jnp.float32)

def square_parts(hidden_in, grads_in, owner_in, first_example):
    hidden_gram = jnp.dot(hidden_in, hidden_in.T, preferred_element_type=jnp.float32)
    grad_gram = jnp.dot(grads_in, grads_in.T, preferred_element_type=jnp.float32)
    matched = (owner_in[:, None] == owner_in[None, :]).astype(jnp.float32)
    row_sums = lax.optimization_barrier(jnp.sum(hidden_gram * grad_gram * matched, axis=1))
    return lax.optimization_barrier(jnp.sum(row_sums[:, None] * belongs_to(owner_in, first_example), axis=0))

def reference(hidden, grad_out, gate_weights, routes, example_ids):
    threshold = math.sqrt(FFW * DW * TOK_DEV * (0.43 + 0.01 * TOK_DEV))
    grad_rows = (gate_weights[:, :, None] * grad_out[:, None, :].astype(jnp.float32)).astype(jnp.bfloat16)
    hidden_all = hidden.reshape(N_DP, N_EXPERT, TOK_DEV, 2, FFW)
    grads_all = grad_rows.reshape(N_DP, N_EXPERT, TOK_DEV, 2, DW)
    routes_all = routes.reshape(N_DP, N_EXPERT, TOK_DEV, 2)
    ids_all = example_ids.reshape(N_DP, N_EXPERT, TOK_DEV)
    replicas = jnp.arange(N_DP, dtype=jnp.int32)

    def row_norms(inputs):
        replica, hidden_row, grads_row, routes_row, ids_row = inputs
        hidden_in, grads_in, owner_in = gather_row(hidden_row, grads_row, routes_row, ids_row)
        first_example = replica * EX_BLK
        parts = lax.map(lambda packed: square_parts(packed[0], packed[1], packed[2], first_example), (hidden_in, grads_in, owner_in))
        return lax.optimization_barrier(jnp.sum(parts, axis=0))
    squares = lax.map(row_norms, (replicas, hidden_all, grads_all, routes_all, ids_all)).reshape(EXAMPLES)
    norm_values = jnp.sqrt(squares)
    factors = jnp.minimum(1.0, threshold / norm_values)

    def add_row(running, inputs):
        replica, hidden_row, grads_row, routes_row, ids_row = inputs
        hidden_in, grads_in, owner_in = gather_row(hidden_row, grads_row, routes_row, ids_row)
        first_example = replica * EX_BLK
        block_factors = lax.dynamic_slice(factors, (first_example,), (EX_BLK,))

        def one_expert(packed):
            row_factors = lax.optimization_barrier(jnp.sum(belongs_to(packed[2], first_example) * block_factors[None, :], axis=1))
            clipped = (row_factors[:, None] * packed[1].astype(jnp.float32)).astype(jnp.bfloat16)
            return jnp.dot(packed[0].T, clipped, preferred_element_type=jnp.float32).astype(jnp.bfloat16)
        partials = lax.map(one_expert, (hidden_in, grads_in, owner_in))
        partials = lax.optimization_barrier(partials)
        return (running + partials.astype(jnp.float32), None)
    running, unused = lax.scan(add_row, jnp.zeros((EXPERTS, FFW, DW), jnp.float32), (replicas, hidden_all, grads_all, routes_all, ids_all))
    update = (running / EXAMPLES).astype(jnp.bfloat16)
    return (update, norm_values / threshold)
```

```python
import math

import jax
import jax.numpy as jnp
from jax import lax
from jax.experimental import pallas as pl
from jax.experimental.pallas import tpu as pltpu
from jax.sharding import PartitionSpec as P

MESH = pl.DeviceIdType.MESH
BF16, F32 = jnp.bfloat16, jnp.float32

SIDE = 4
EXPERTS = 8
EX_BLK = 8
LANES = 128
TILE = 512


def _dot(a, b):
    return lax.dot_general(a, b, (((1,), (0,)), ((), ())), preferred_element_type=F32)


def _dot_t(a, b):
    return lax.dot_general(a, b, (((1,), (1,)), ((), ())), preferred_element_type=F32)


def kernel(
    small, hid, grad, out, norm_out,
    hv, hp, gv, gs, hs, gall, hin, hg, ht, oh, hgram, mgram, rowf,
    sq_send, sq_recv, f_send, f_recv, part_a, part_b, part_c, part_in, own,
    in_sem, z_send, z_recv, fg_send, fg_recv, fh_send, fh_recv,
    sq_ssem, sq_rsem, f_ssem, f_rsem, rs_send, rs_recv,
):
    tokens, _, width = hid.shape
    out_width = grad.shape[1]
    cap = 3 * tokens // EXPERTS
    rows = EXPERTS * cap
    half = rows // 2
    slice_w = width // SIDE
    chunk = slice_w // SIDE
    hc = chunk // 2
    threshold = math.sqrt(width * out_width * tokens * (0.43 + 0.01 * tokens))

    dp, ex = lax.axis_index("dp"), lax.axis_index("expert")
    x, y = lax.div(dp, SIDE), lax.rem(dp, SIDE)
    z, c = lax.div(ex, 2), lax.rem(ex, 2)
    gpos = y + c * (x - y)
    rpos = x + c * (y - x)

    def along(d, turned):
        a = x * SIDE + lax.rem(y + d, SIDE)
        b = lax.rem(x + d, SIDE) * SIDE + y
        return (a + turned * (b - a), ex)

    def gather_peer(d):
        return along(d, c)

    def sum_peer(d):
        return along(d, 1 - c)

    zsteps = [(2, 0), (2, 1), (1, 0), (3, 0), (1, 1), (3, 1), (0, 1)]

    def z_peer(dz, dc):
        pz = lax.rem(z + dz, SIDE)
        pc = c if dc == 0 else 1 - c
        return pz, pc

    g_in = pltpu.make_async_copy(grad, gv, in_sem.at[0])
    h_in = pltpu.make_async_copy(hid, hv, in_sem.at[1])
    g_in.start()
    h_in.start()

    barrier = pltpu.get_barrier_semaphore()
    peers = []
    for dz, dc in zsteps:
        pz, pc = z_peer(dz, dc)
        peers.append((dp, pz * 2 + pc))
    for d in (1, 2, 3):
        peers.append(gather_peer(d))
    for d in (1, 3):
        peers.append(sum_peer(d))
    for peer in peers:
        pl.semaphore_signal(barrier, inc=1, device_id=peer, device_id_type=MESH)

    pairs = 2 * tokens
    route = small[0:1, :]
    gate = small[1:2, :]
    local_id = small[2:3, :] - (dp * EX_BLK).astype(F32)
    expert_of = lax.broadcasted_iota(jnp.int32, (EXPERTS, pairs), 0)
    chosen = route == expert_of.astype(F32)
    before = lax.broadcasted_iota(jnp.int32, (pairs, pairs), 0) < lax.broadcasted_iota(
        jnp.int32, (pairs, pairs), 1
    )
    place = _dot(
        jnp.where(chosen, 1.0, 0.0).astype(BF16), jnp.where(before, 1.0, 0.0).astype(BF16)
    )
    base = (lax.rem(expert_of, 2) * half + lax.div(expert_of, 2) * cap).astype(F32)
    slot = jnp.sum(jnp.where(chosen, base + place, 0.0), axis=0, keepdims=True)
    hit = slot == lax.broadcasted_iota(jnp.int32, (rows, pairs), 0).astype(F32)
    onehot = jnp.where(hit, 1.0, 0.0).astype(BF16)
    oh[...] = onehot
    to_token = jnp.where(
        lax.div(lax.broadcasted_iota(jnp.int32, (pairs, tokens), 0), 2)
        == lax.broadcasted_iota(jnp.int32, (pairs, tokens), 1),
        1.0,
        0.0,
    ).astype(BF16)
    token_hot = _dot(onehot, to_token).astype(BF16)
    slot_gate = jnp.sum(jnp.where(hit, gate, 0.0), axis=1, keepdims=True)
    slot_id = jnp.sum(jnp.where(hit, local_id + 1.0, 0.0), axis=1, keepdims=True) - 1.0
    lane = lax.broadcasted_iota(jnp.int32, (rows, LANES), 1).astype(F32)
    gs[:, out_width:] = jnp.where(slot_id == lane, 1.0, 0.0).astype(BF16)
    g_in.wait()
    for n in range(out_width // TILE):
        cols = slice(n * TILE, (n + 1) * TILE)
        gs[:, cols] = (slot_gate * _dot(token_hot, gv[:, cols])).astype(BF16)

    pl.semaphore_wait(barrier, len(peers))

    my_rows = pl.ds(pl.multiple_of(ex * cap, 16), cap)
    my_grad_rows = pl.ds(pl.multiple_of(3 * rows + ex * cap, 16), cap)

    def block(pz, pc):
        return pl.ds(pl.multiple_of(pc * half + pz * cap, 16), cap)

    def z_copies(k):
        copies = []
        for i, (dz, dc) in enumerate(zsteps):
            pz, pc = z_peer(dz, dc)
            if k == 0:
                src, dst = gs.at[block(pz, pc)], gall.at[my_grad_rows]
            else:
                src, dst = hs.at[k - 1, block(pz, pc)], hin.at[k - 1, my_rows]
            copies.append(
                pltpu.make_async_remote_copy(
                    src_ref=src,
                    dst_ref=dst,
                    send_sem=z_send.at[k, i],
                    recv_sem=z_recv.at[k, i],
                    device_id=(dp, pz * 2 + pc),
                    device_id_type=MESH,
                )
            )
        return copies

    zc = [z_copies(k) for k in range(1 + SIDE)]
    for copy in zc[0]:
        copy.start()
    gall[my_grad_rows, :] = gs[block(z, c), :]

    h_in.wait()
    for j in range(SIDE):
        for a in range(SIDE // 2):
            first, second = (2 * a * SIDE + j) * chunk, ((2 * a + 1) * SIDE + j) * chunk
            pair = jnp.concatenate(
                [
                    hv[:, :, first : first + chunk].reshape(pairs, chunk),
                    hv[:, :, second : second + chunk].reshape(pairs, chunk),
                ],
                axis=1,
            )
            at = j * slice_w + 2 * a * chunk
            hp[:, at : at + 2 * chunk] = pair

    def pack(q):
        je = pl.ds(pl.multiple_of(lax.rem(y + 1 + q, SIDE) * slice_w, LANES), slice_w)
        jo = pl.ds(pl.multiple_of(lax.rem(x + 1 + q, SIDE) * slice_w, LANES), slice_w)
        hs[q, 0:half, :] = _dot(oh[0:half, :], hp[:, je]).astype(BF16)
        hs[q, half:rows, :] = _dot(
            oh[half:rows, :], hv[:, :, jo].reshape(pairs, slice_w)
        ).astype(BF16)

    def forward_grads(d):
        return pltpu.make_async_remote_copy(
            src_ref=gall.at[3 * rows : 4 * rows],
            dst_ref=gall.at[(d - 1) * rows : d * rows],
            send_sem=fg_send.at[d - 1],
            recv_sem=fg_recv.at[d - 1],
            device_id=gather_peer(d),
            device_id_type=MESH,
        )

    def forward_hidden(q):
        return pltpu.make_async_remote_copy(
            src_ref=hin.at[q],
            dst_ref=hg.at[q],
            send_sem=fh_send.at[q],
            recv_sem=fh_recv.at[q],
            device_id=gather_peer(q + 1),
            device_id_type=MESH,
        )

    fgs = [forward_grads(d) for d in (1, 2, 3)]
    fhs = [forward_hidden(q) for q in range(SIDE - 1)]

    for k in range(1 + SIDE):
        if k < SIDE:
            pack(k)
            for copy in zc[k + 1]:
                copy.start()
            hin[k, my_rows, :] = hs[k, block(z, c), :]
        for copy in zc[k]:
            copy.wait_recv()
        if k == 0:
            for copy in fgs:
                copy.start()
            g = gall[3 * rows : 4 * rows, 0:out_width]
            b = gall[3 * rows : 4 * rows, out_width:]
            mgram[...] = _dot_t(g, g) * _dot_t(b, b)
        else:
            if k < SIDE:
                fhs[k - 1].start()
            h = hin[k - 1]
            gram = _dot_t(h, h)
            if k > 1:
                gram = gram + hgram[...]
            if k < SIDE:
                hgram[...] = gram
            else:
                row_sums = jnp.sum(gram * mgram[...], axis=1, keepdims=True)
                member = gall[3 * rows : 4 * rows, out_width:].astype(F32)
                part = jnp.sum(row_sums * member, axis=0, keepdims=True)
                sq_send[...] = jnp.broadcast_to(part, (8, LANES))

    sq_copies = []
    for i, (dz, dc) in enumerate(zsteps):
        pz, pc = z_peer(dz, dc)
        sq_copies.append(
            pltpu.make_async_remote_copy(
                src_ref=sq_send,
                dst_ref=sq_recv.at[i],
                send_sem=sq_ssem.at[i],
                recv_sem=sq_rsem.at[i],
                device_id=(dp, pz * 2 + pc),
                device_id_type=MESH,
            )
        )
    for copy in sq_copies:
        copy.start()
    ht[:, 3 * rows : 4 * rows] = hin[SIDE - 1].T
    total = sq_send[...]
    for i, copy in enumerate(sq_copies):
        copy.wait_recv()
        total = total + sq_recv[i]
    norms = jnp.sqrt(total)
    norm_out[...] = norms[0:1, 0:EX_BLK] / threshold
    f_send[...] = jnp.minimum(1.0, threshold / norms)
    f_copies = []
    for d in (1, 2, 3):
        f_copies.append(
            pltpu.make_async_remote_copy(
                src_ref=f_send,
                dst_ref=f_recv.at[d - 1],
                send_sem=f_ssem.at[d - 1],
                recv_sem=f_rsem.at[d - 1],
                device_id=gather_peer(d),
                device_id_type=MESH,
            )
        )
    for copy in f_copies:
        copy.start()
    for q in range(SIDE - 1):
        fhs[q].wait_recv()
        ht[:, q * rows : (q + 1) * rows] = hg[q].T
    for copy in fgs:
        copy.wait_recv()
        copy.wait_send()
    for copy in f_copies:
        copy.wait_recv()
    for q in range(SIDE):
        span = slice(q * rows, (q + 1) * rows)
        factors = f_send[0:1, :] if q == SIDE - 1 else f_recv[q, 0:1, :]
        row_factor = jnp.sum(
            gall[span, out_width:].astype(F32) * factors, axis=1, keepdims=True
        )
        rowf[span, :] = jnp.broadcast_to(row_factor, (rows, LANES))

    def chunk_rows(d, lower, size):
        start = lax.rem(rpos + d, SIDE) * chunk + lower * hc
        return pl.ds(pl.multiple_of(start, 32), size)

    def tile_at(n):
        return pl.ds(pl.multiple_of(n * TILE, TILE), TILE)

    def rs_copy(slot_, n):
        src = (
            part_a.at[0:hc],
            part_b.at[0],
            part_c.at[0],
            part_a.at[hc:chunk],
            part_b.at[1],
            part_c.at[1],
        )[slot_]
        return pltpu.make_async_remote_copy(
            src_ref=src.at[:, tile_at(n)],
            dst_ref=part_in.at[slot_, :, tile_at(n)],
            send_sem=rs_send.at[slot_, n],
            recv_sem=rs_recv.at[slot_, n],
            device_id=sum_peer(1 if slot_ < 3 else 3),
            device_id_type=MESH,
        )

    tiles = out_width // TILE

    @pl.loop(0, tiles)
    def _(n):
        cols = tile_at(n)
        wide = jnp.concatenate([rowf[...]] * (TILE // LANES), axis=1)
        gall[:, cols] = (wide * gall[:, cols].astype(F32)).astype(BF16)
        part_a[:, cols] = _dot(ht[chunk_rows(2, 0, chunk), :], gall[:, cols]).astype(BF16)
        rs_copy(0, n).start()
        rs_copy(3, n).start()

    @pl.loop(0, tiles)
    def _(n):
        cols = tile_at(n)
        part_b[0, :, cols] = _dot(ht[chunk_rows(1, 1, hc), :], gall[:, cols]).astype(BF16)
        rs_copy(1, n).start()
        part_b[1, :, cols] = _dot(ht[chunk_rows(3, 0, hc), :], gall[:, cols]).astype(BF16)
        rs_copy(4, n).start()

    @pl.loop(0, tiles)
    def _(n):
        cols = tile_at(n)
        term = _dot(ht[chunk_rows(1, 0, hc), :], gall[:, cols])
        rs_copy(0, n).wait_recv()
        part_c[0, :, cols] = (term + part_in[0, :, cols].astype(F32)).astype(BF16)
        rs_copy(2, n).start()
        term = _dot(ht[chunk_rows(3, 1, hc), :], gall[:, cols])
        rs_copy(3, n).wait_recv()
        part_c[1, :, cols] = (term + part_in[3, :, cols].astype(F32)).astype(BF16)
        rs_copy(5, n).start()

    @pl.loop(0, tiles)
    def _(n):
        cols = tile_at(n)
        own[:, cols] = _dot(ht[chunk_rows(0, 0, chunk), :], gall[:, cols])

    scale = 1.0 / (EX_BLK * SIDE * SIDE)

    @pl.loop(0, tiles)
    def _(n):
        cols = tile_at(n)
        for slot_ in (1, 2, 4, 5):
            rs_copy(slot_, n).wait_recv()
        upper = own[0:hc, cols] + part_in[2, :, cols].astype(F32) + part_in[4, :, cols].astype(F32)
        lower = own[hc:chunk, cols] + part_in[1, :, cols].astype(F32) + part_in[5, :, cols].astype(F32)
        out[0:hc, cols] = (upper * scale).astype(BF16)
        out[hc:chunk, cols] = (lower * scale).astype(BF16)

    for copies in zc:
        for copy in copies:
            copy.wait_send()
    for copy in fhs + sq_copies + f_copies:
        copy.wait_send()

    @pl.loop(0, tiles)
    def _(n):
        for slot_ in range(6):
            rs_copy(slot_, n).wait_send()


def body(hidden, grad_out, gate_weights, routes, example_ids):
    tokens, _, width = hidden.shape
    out_width = grad_out.shape[1]
    rows = 3 * tokens
    slice_w = width // SIDE
    chunk = slice_w // SIDE
    hc = chunk // 2
    wide = out_width + LANES
    tiles = out_width // TILE
    small = jnp.stack(
        [
            routes.reshape(-1).astype(F32),
            gate_weights.reshape(-1),
            jnp.repeat(example_ids, 2).astype(F32),
        ]
    )
    vmem = pl.BlockSpec(memory_space=pltpu.VMEM)
    hbm = pl.BlockSpec(memory_space=pl.ANY)
    dma = pltpu.SemaphoreType.DMA
    update, norms = pl.pallas_call(
        kernel,
        out_shape=(
            jax.ShapeDtypeStruct((chunk, out_width), BF16),
            jax.ShapeDtypeStruct((1, EX_BLK), F32),
        ),
        in_specs=[vmem, hbm, hbm],
        out_specs=(vmem, vmem),
        scratch_shapes=[
            pltpu.VMEM((tokens, 2, width), BF16),
            pltpu.VMEM((2 * tokens, width), BF16),
            pltpu.VMEM((tokens, out_width), BF16),
            pltpu.VMEM((rows, wide), BF16),
            pltpu.VMEM((SIDE, rows, slice_w), BF16),
            pltpu.VMEM((SIDE * rows, wide), BF16),
            pltpu.VMEM((SIDE, rows, slice_w), BF16),
            pltpu.VMEM((SIDE - 1, rows, slice_w), BF16),
            pltpu.VMEM((slice_w, SIDE * rows), BF16),
            pltpu.VMEM((rows, 2 * tokens), BF16),
            pltpu.VMEM((rows, rows), F32),
            pltpu.VMEM((rows, rows), F32),
            pltpu.VMEM((SIDE * rows, LANES), F32),
            pltpu.VMEM((8, LANES), F32),
            pltpu.VMEM((EXPERTS - 1, 8, LANES), F32),
            pltpu.VMEM((8, LANES), F32),
            pltpu.VMEM((SIDE - 1, 8, LANES), F32),
            pltpu.VMEM((chunk, out_width), BF16),
            pltpu.VMEM((2, hc, out_width), BF16),
            pltpu.VMEM((2, hc, out_width), BF16),
            pltpu.VMEM((6, hc, out_width), BF16),
            pltpu.VMEM((chunk, out_width), F32),
            dma((2,)),
            dma((1 + SIDE, EXPERTS - 1)),
            dma((1 + SIDE, EXPERTS - 1)),
            dma((SIDE - 1,)),
            dma((SIDE - 1,)),
            dma((SIDE - 1,)),
            dma((SIDE - 1,)),
            dma((EXPERTS - 1,)),
            dma((EXPERTS - 1,)),
            dma((SIDE - 1,)),
            dma((SIDE - 1,)),
            dma((6, tiles)),
            dma((6, tiles)),
        ],
        compiler_params=pltpu.CompilerParams(
            collective_id=0, has_side_effects=True, vmem_limit_bytes=60 * 1024 * 1024
        ),
    )(small, hidden, grad_out)
    return update[None], norms.reshape(EX_BLK)


def solution(mesh):
    return jax.shard_map(
        body,
        mesh=mesh,
        in_specs=(
            P(("dp", "expert"), None, None),
            P(("dp", "expert"), None),
            P(("dp", "expert"), None),
            P(("dp", "expert"), None),
            P(("dp", "expert")),
        ),
        out_specs=(P("expert", "dp", None), P("dp")),
        check_vma=False,
    )
```

```python
import math

import jax
import jax.numpy as jnp
from jax import lax
from jax.experimental import pallas as pl
from jax.experimental.pallas import tpu as pltpu
from jax.sharding import PartitionSpec as P

MESH = pl.DeviceIdType.MESH
BF16, F32 = jnp.bfloat16, jnp.float32

SIDE = 4
EXPERTS = 8
EX_BLK = 8
LANES = 128
TILE = 512


def _dot(a, b):
    return lax.dot_general(a, b, (((1,), (0,)), ((), ())), preferred_element_type=F32)


def _dot_t(a, b):
    return lax.dot_general(a, b, (((1,), (1,)), ((), ())), preferred_element_type=F32)


def kernel(
    routes, gates, ids, hid, grad, out, norm_out,
    hv, hp, gv, gs, hs, gall, hin, hg, ht, oh, hgram, mgram, rowf,
    sq_send, sq_recv, f_send, f_recv, part_a, part_b, part_c, part_in, own,
    in_sem, z_send, z_recv, fg_send, fg_recv, fh_send, fh_recv,
    sq_ssem, sq_rsem, f_ssem, f_rsem, rs_send, rs_recv,
):
    tokens, _, width = hid.shape
    out_width = grad.shape[1]
    cap = 3 * tokens // EXPERTS
    rows = EXPERTS * cap
    half = rows // 2
    slice_w = width // SIDE
    chunk = slice_w // SIDE
    hc = chunk // 2
    g_cols = ((0, out_width // 2), (out_width // 2, out_width + LANES))
    threshold = math.sqrt(width * out_width * tokens * (0.43 + 0.01 * tokens))

    dp, ex = lax.axis_index("dp"), lax.axis_index("expert")
    x, y = lax.div(dp, SIDE), lax.rem(dp, SIDE)
    z, c = lax.div(ex, 2), lax.rem(ex, 2)
    gpos = y + c * (x - y)
    rpos = x + c * (y - x)

    def along(d, turned):
        a = x * SIDE + lax.rem(y + d, SIDE)
        b = lax.rem(x + d, SIDE) * SIDE + y
        return (a + turned * (b - a), ex)

    def gather_peer(d):
        return along(d, c)

    def sum_peer(d):
        return along(d, 1 - c)

    zsteps = [(2, 0), (2, 1), (1, 0), (3, 0), (1, 1), (3, 1), (0, 1)]

    def z_peer(dz, dc):
        pz = lax.rem(z + dz, SIDE)
        pc = c if dc == 0 else 1 - c
        return pz, pc

    g_in = pltpu.make_async_copy(grad, gv, in_sem.at[0])
    h_in = pltpu.make_async_copy(hid, hv, in_sem.at[1])
    g_in.start()
    h_in.start()

    barrier = pltpu.get_barrier_semaphore()
    peers = []
    for dz, dc in zsteps:
        pz, pc = z_peer(dz, dc)
        peers.append((dp, pz * 2 + pc))
    for d in (1, 2, 3):
        peers.append(gather_peer(d))
    for d in (1, 3):
        peers.append(sum_peer(d))
    for peer in peers:
        pl.semaphore_signal(barrier, inc=1, device_id=peer, device_id_type=MESH)

    pairs = 2 * tokens
    route = jnp.concatenate([routes[0:1, :], routes[1:2, :]], axis=1)
    gate = jnp.concatenate([gates[0:1, :], gates[1:2, :]], axis=1)
    local_id = (ids[0:1, :] - dp * EX_BLK).astype(F32)
    local_id = jnp.concatenate([local_id, local_id], axis=1)
    expert_of = lax.broadcasted_iota(jnp.int32, (EXPERTS, pairs), 0)
    chosen = route == expert_of
    before = lax.broadcasted_iota(jnp.int32, (pairs, pairs), 0) < lax.broadcasted_iota(
        jnp.int32, (pairs, pairs), 1
    )
    place = _dot(
        jnp.where(chosen, 1.0, 0.0).astype(BF16), jnp.where(before, 1.0, 0.0).astype(BF16)
    )
    base = (lax.rem(expert_of, 2) * half + lax.div(expert_of, 2) * cap).astype(F32)
    slot = jnp.sum(jnp.where(chosen, base + place, 0.0), axis=0, keepdims=True)
    hit = slot == lax.broadcasted_iota(jnp.int32, (rows, pairs), 0).astype(F32)
    hot = jnp.where(hit, 1.0, 0.0)
    token_hot = (hot[:, 0:tokens] + hot[:, tokens:]).astype(BF16)
    slot_gate = jnp.sum(jnp.where(hit, gate, 0.0), axis=1, keepdims=True)

    def pack_grads(first, last):
        for n in range(first // TILE, last // TILE):
            cols = slice(n * TILE, (n + 1) * TILE)
            gs[:, cols] = (slot_gate * _dot(token_hot, gv[:, cols])).astype(BF16)

    g_in.wait()
    pack_grads(*g_cols[0])
    pl.semaphore_wait(barrier, len(peers))

    my_rows = pl.ds(pl.multiple_of(ex * cap, 16), cap)
    my_grad_rows = pl.ds(pl.multiple_of(3 * rows + ex * cap, 16), cap)

    def block(pz, pc):
        return pl.ds(pl.multiple_of(pc * half + pz * cap, 16), cap)

    def z_copies(k):
        copies = []
        for i, (dz, dc) in enumerate(zsteps):
            pz, pc = z_peer(dz, dc)
            if k < 2:
                cols = slice(*g_cols[k])
                src, dst = gs.at[block(pz, pc), cols], gall.at[my_grad_rows, cols]
            else:
                src, dst = hs.at[k - 2, block(pz, pc)], hin.at[k - 2, my_rows]
            copies.append(
                pltpu.make_async_remote_copy(
                    src_ref=src,
                    dst_ref=dst,
                    send_sem=z_send.at[k, i],
                    recv_sem=z_recv.at[k, i],
                    device_id=(dp, pz * 2 + pc),
                    device_id_type=MESH,
                )
            )
        return copies

    zc = [z_copies(k) for k in range(2 + SIDE)]
    for copy in zc[0]:
        copy.start()

    pack_grads(*g_cols[1])
    slot_id = jnp.sum(jnp.where(hit, local_id + 1.0, 0.0), axis=1, keepdims=True) - 1.0
    lane = lax.broadcasted_iota(jnp.int32, (rows, LANES), 1).astype(F32)
    gs[:, out_width:] = jnp.where(slot_id == lane, 1.0, 0.0).astype(BF16)
    for copy in zc[1]:
        copy.start()
    gall[my_grad_rows, :] = gs[block(z, c), :]

    from_pair = lax.broadcasted_iota(jnp.int32, (pairs, pairs), 0)
    to_pair = lax.broadcasted_iota(jnp.int32, (pairs, pairs), 1)
    interleave = 2 * lax.rem(from_pair, tokens) + lax.div(from_pair, tokens) == to_pair
    oh[...] = _dot(
        hot.astype(BF16), jnp.where(interleave, 1.0, 0.0).astype(BF16)
    ).astype(BF16)

    h_in.wait()
    for j in range(SIDE):
        for a in range(SIDE // 2):
            first, second = (2 * a * SIDE + j) * chunk, ((2 * a + 1) * SIDE + j) * chunk
            pair = jnp.concatenate(
                [
                    hv[:, :, first : first + chunk].reshape(pairs, chunk),
                    hv[:, :, second : second + chunk].reshape(pairs, chunk),
                ],
                axis=1,
            )
            at = j * slice_w + 2 * a * chunk
            hp[:, at : at + 2 * chunk] = pair

    def pack(q):
        je = pl.ds(pl.multiple_of(lax.rem(y + 1 + q, SIDE) * slice_w, LANES), slice_w)
        jo = pl.ds(pl.multiple_of(lax.rem(x + 1 + q, SIDE) * slice_w, LANES), slice_w)
        hs[q, 0:half, :] = _dot(oh[0:half, :], hp[:, je]).astype(BF16)
        hs[q, half:rows, :] = _dot(
            oh[half:rows, :], hv[:, :, jo].reshape(pairs, slice_w)
        ).astype(BF16)

    def forward_grads(k, d):
        cols = slice(*g_cols[k])
        return pltpu.make_async_remote_copy(
            src_ref=gall.at[3 * rows : 4 * rows, cols],
            dst_ref=gall.at[(d - 1) * rows : d * rows, cols],
            send_sem=fg_send.at[k, d - 1],
            recv_sem=fg_recv.at[k, d - 1],
            device_id=gather_peer(d),
            device_id_type=MESH,
        )

    def forward_hidden(q):
        return pltpu.make_async_remote_copy(
            src_ref=hin.at[q],
            dst_ref=hg.at[q],
            send_sem=fh_send.at[q],
            recv_sem=fh_recv.at[q],
            device_id=gather_peer(q + 1),
            device_id_type=MESH,
        )

    fgs = [[forward_grads(k, d) for d in (1, 2, 3)] for k in range(2)]
    fhs = [forward_hidden(q) for q in range(SIDE - 1)]

    for k in range(2 + SIDE):
        q = k - 2
        if 1 <= k < 1 + SIDE:
            pack(q + 1)
            for copy in zc[k + 1]:
                copy.start()
            hin[q + 1, my_rows, :] = hs[q + 1, block(z, c), :]
        for copy in zc[k]:
            copy.wait_recv()
        if k < 2:
            for copy in fgs[k]:
                copy.start()
            if k == 1:
                g = gall[3 * rows : 4 * rows, 0:out_width]
                b = gall[3 * rows : 4 * rows, out_width:]
                mgram[...] = _dot_t(g, g) * _dot_t(b, b)
        else:
            if q < SIDE - 1:
                fhs[q].start()
            h = hin[q]
            gram = _dot_t(h, h)
            if q > 0:
                gram = gram + hgram[...]
            if q < SIDE - 1:
                hgram[...] = gram
            else:
                row_sums = jnp.sum(gram * mgram[...], axis=1, keepdims=True)
                member = gall[3 * rows : 4 * rows, out_width:].astype(F32)
                part = jnp.sum(row_sums * member, axis=0, keepdims=True)
                sq_send[...] = jnp.broadcast_to(part, (8, LANES))

    sq_copies = []
    for i, (dz, dc) in enumerate(zsteps):
        pz, pc = z_peer(dz, dc)
        sq_copies.append(
            pltpu.make_async_remote_copy(
                src_ref=sq_send,
                dst_ref=sq_recv.at[i],
                send_sem=sq_ssem.at[i],
                recv_sem=sq_rsem.at[i],
                device_id=(dp, pz * 2 + pc),
                device_id_type=MESH,
            )
        )
    for copy in sq_copies:
        copy.start()
    ht[:, 3 * rows : 4 * rows] = hin[SIDE - 1].T
    total = sq_send[...]
    for i, copy in enumerate(sq_copies):
        copy.wait_recv()
        total = total + sq_recv[i]
    norms = jnp.sqrt(total)
    norm_out[...] = norms[0:1, 0:EX_BLK] / threshold
    f_send[...] = jnp.minimum(1.0, threshold / norms)
    f_copies = []
    for d in (1, 2, 3):
        f_copies.append(
            pltpu.make_async_remote_copy(
                src_ref=f_send,
                dst_ref=f_recv.at[d - 1],
                send_sem=f_ssem.at[d - 1],
                recv_sem=f_rsem.at[d - 1],
                device_id=gather_peer(d),
                device_id_type=MESH,
            )
        )
    for copy in f_copies:
        copy.start()
    for q in range(SIDE - 1):
        fhs[q].wait_recv()
        ht[:, q * rows : (q + 1) * rows] = hg[q].T
    for copy in fgs[0] + fgs[1]:
        copy.wait_recv()
        copy.wait_send()
    for copy in f_copies:
        copy.wait_recv()
    for q in range(SIDE):
        span = slice(q * rows, (q + 1) * rows)
        factors = f_send[0:1, :] if q == SIDE - 1 else f_recv[q, 0:1, :]
        row_factor = jnp.sum(
            gall[span, out_width:].astype(F32) * factors, axis=1, keepdims=True
        )
        rowf[span, :] = jnp.broadcast_to(row_factor, (rows, LANES))

    def chunk_rows(d, lower, size):
        start = lax.rem(rpos + d, SIDE) * chunk + lower * hc
        return pl.ds(pl.multiple_of(start, 32), size)

    def tile_at(n):
        return pl.ds(pl.multiple_of(n * TILE, TILE), TILE)

    def rs_copy(slot_, n):
        src = (
            part_a.at[0:hc],
            part_b.at[0],
            part_c.at[0],
            part_a.at[hc:chunk],
            part_b.at[1],
            part_c.at[1],
        )[slot_]
        return pltpu.make_async_remote_copy(
            src_ref=src.at[:, tile_at(n)],
            dst_ref=part_in.at[slot_, :, tile_at(n)],
            send_sem=rs_send.at[slot_, n],
            recv_sem=rs_recv.at[slot_, n],
            device_id=sum_peer(1 if slot_ < 3 else 3),
            device_id_type=MESH,
        )

    tiles = out_width // TILE

    @pl.loop(0, tiles)
    def _(n):
        cols = tile_at(n)
        wide = jnp.concatenate([rowf[...]] * (TILE // LANES), axis=1)
        gall[:, cols] = (wide * gall[:, cols].astype(F32)).astype(BF16)
        part_a[:, cols] = _dot(ht[chunk_rows(2, 0, chunk), :], gall[:, cols]).astype(BF16)
        rs_copy(0, n).start()
        rs_copy(3, n).start()

    @pl.loop(0, tiles)
    def _(n):
        cols = tile_at(n)
        part_b[0, :, cols] = _dot(ht[chunk_rows(1, 1, hc), :], gall[:, cols]).astype(BF16)
        rs_copy(1, n).start()
        part_b[1, :, cols] = _dot(ht[chunk_rows(3, 0, hc), :], gall[:, cols]).astype(BF16)
        rs_copy(4, n).start()

    @pl.loop(0, tiles)
    def _(n):
        cols = tile_at(n)
        term = _dot(ht[chunk_rows(1, 0, hc), :], gall[:, cols])
        rs_copy(0, n).wait_recv()
        part_c[0, :, cols] = (term + part_in[0, :, cols].astype(F32)).astype(BF16)
        rs_copy(2, n).start()
        term = _dot(ht[chunk_rows(3, 1, hc), :], gall[:, cols])
        rs_copy(3, n).wait_recv()
        part_c[1, :, cols] = (term + part_in[3, :, cols].astype(F32)).astype(BF16)
        rs_copy(5, n).start()

    @pl.loop(0, tiles)
    def _(n):
        cols = tile_at(n)
        own[:, cols] = _dot(ht[chunk_rows(0, 0, chunk), :], gall[:, cols])

    scale = 1.0 / (EX_BLK * SIDE * SIDE)

    @pl.loop(0, tiles)
    def _(n):
        cols = tile_at(n)
        for slot_ in (1, 2, 4, 5):
            rs_copy(slot_, n).wait_recv()
        upper = own[0:hc, cols] + part_in[2, :, cols].astype(F32) + part_in[4, :, cols].astype(F32)
        lower = own[hc:chunk, cols] + part_in[1, :, cols].astype(F32) + part_in[5, :, cols].astype(F32)
        out[0:hc, cols] = (upper * scale).astype(BF16)
        out[hc:chunk, cols] = (lower * scale).astype(BF16)

    for copies in zc:
        for copy in copies:
            copy.wait_send()
    for copy in fhs + sq_copies + f_copies:
        copy.wait_send()

    @pl.loop(0, tiles)
    def _(n):
        for slot_ in range(6):
            rs_copy(slot_, n).wait_send()


def body(hidden, grad_out, gate_weights, routes, example_ids):
    tokens, _, width = hidden.shape
    out_width = grad_out.shape[1]
    rows = 3 * tokens
    slice_w = width // SIDE
    chunk = slice_w // SIDE
    hc = chunk // 2
    wide = out_width + LANES
    tiles = out_width // TILE
    vmem = pl.BlockSpec(memory_space=pltpu.VMEM)
    hbm = pl.BlockSpec(memory_space=pl.ANY)
    dma = pltpu.SemaphoreType.DMA
    update, norms = pl.pallas_call(
        kernel,
        out_shape=(
            jax.ShapeDtypeStruct((chunk, out_width), BF16),
            jax.ShapeDtypeStruct((1, EX_BLK), F32),
        ),
        in_specs=[vmem, vmem, vmem, hbm, hbm],
        out_specs=(vmem, vmem),
        scratch_shapes=[
            pltpu.VMEM((tokens, 2, width), BF16),
            pltpu.VMEM((2 * tokens, width), BF16),
            pltpu.VMEM((tokens, out_width), BF16),
            pltpu.VMEM((rows, wide), BF16),
            pltpu.VMEM((SIDE, rows, slice_w), BF16),
            pltpu.VMEM((SIDE * rows, wide), BF16),
            pltpu.VMEM((SIDE, rows, slice_w), BF16),
            pltpu.VMEM((SIDE - 1, rows, slice_w), BF16),
            pltpu.VMEM((slice_w, SIDE * rows), BF16),
            pltpu.VMEM((rows, 2 * tokens), BF16),
            pltpu.VMEM((rows, rows), F32),
            pltpu.VMEM((rows, rows), F32),
            pltpu.VMEM((SIDE * rows, LANES), F32),
            pltpu.VMEM((8, LANES), F32),
            pltpu.VMEM((EXPERTS - 1, 8, LANES), F32),
            pltpu.VMEM((8, LANES), F32),
            pltpu.VMEM((SIDE - 1, 8, LANES), F32),
            pltpu.VMEM((chunk, out_width), BF16),
            pltpu.VMEM((2, hc, out_width), BF16),
            pltpu.VMEM((2, hc, out_width), BF16),
            pltpu.VMEM((6, hc, out_width), BF16),
            pltpu.VMEM((chunk, out_width), F32),
            dma((2,)),
            dma((2 + SIDE, EXPERTS - 1)),
            dma((2 + SIDE, EXPERTS - 1)),
            dma((2, SIDE - 1)),
            dma((2, SIDE - 1)),
            dma((SIDE - 1,)),
            dma((SIDE - 1,)),
            dma((EXPERTS - 1,)),
            dma((EXPERTS - 1,)),
            dma((SIDE - 1,)),
            dma((SIDE - 1,)),
            dma((6, tiles)),
            dma((6, tiles)),
        ],
        compiler_params=pltpu.CompilerParams(
            collective_id=0, has_side_effects=True, vmem_limit_bytes=60 * 1024 * 1024
        ),
    )(routes.T, gate_weights.T, example_ids[None], hidden, grad_out)
    return update[None], norms.reshape(EX_BLK)


def solution(mesh):
    return jax.shard_map(
        body,
        mesh=mesh,
        in_specs=(
            P(("dp", "expert"), None, None),
            P(("dp", "expert"), None),
            P(("dp", "expert"), None),
            P(("dp", "expert"), None),
            P(("dp", "expert")),
        ),
        out_specs=(P("expert", "dp", None), P("dp")),
        check_vma=False,
    )
```

```python
import math

import jax
import jax.numpy as jnp
from jax import lax
from jax.experimental import pallas as pl
from jax.experimental.pallas import tpu as pltpu
from jax.sharding import PartitionSpec as P

MESH = pl.DeviceIdType.MESH
BF16, F32 = jnp.bfloat16, jnp.float32

SIDE = 4
EXPERTS = 8
EX_BLK = 8
LANES = 128
TILE = 512


def _dot(a, b):
    return lax.dot_general(a, b, (((1,), (0,)), ((), ())), preferred_element_type=F32)


def _dot_t(a, b):
    return lax.dot_general(a, b, (((1,), (1,)), ((), ())), preferred_element_type=F32)


def kernel(
    routes, gates, ids, hid, grad, out, norm_out,
    hv, hp, gv, gs, hs, gall, hin, hg, ht, oh, hgram, mgram, rowf,
    sq_send, sq_recv, f_send, f_recv, part_a, part_b, part_c, part_in, own,
    in_sem, z_send, z_recv, fg_send, fg_recv, fh_send, fh_recv,
    sq_ssem, sq_rsem, f_ssem, f_rsem, rs_send, rs_recv,
):
    tokens, _, width = hid.shape
    out_width = grad.shape[1]
    cap = 3 * tokens // EXPERTS
    rows = EXPERTS * cap
    half = rows // 2
    slice_w = width // SIDE
    chunk = slice_w // SIDE
    hc = chunk // 2
    g_cols = ((0, out_width // 2), (out_width // 2, out_width + LANES))
    threshold = math.sqrt(width * out_width * tokens * (0.43 + 0.01 * tokens))

    dp, ex = lax.axis_index("dp"), lax.axis_index("expert")
    x, y = lax.div(dp, SIDE), lax.rem(dp, SIDE)
    z, c = lax.div(ex, 2), lax.rem(ex, 2)
    gpos = y + c * (x - y)
    rpos = x + c * (y - x)

    def along(d, turned):
        a = x * SIDE + lax.rem(y + d, SIDE)
        b = lax.rem(x + d, SIDE) * SIDE + y
        return (a + turned * (b - a), ex)

    def gather_peer(d):
        return along(d, c)

    def sum_peer(d):
        return along(d, 1 - c)

    zsteps = [(2, 0), (2, 1), (1, 0), (3, 0), (1, 1), (3, 1), (0, 1)]

    def z_peer(dz, dc):
        pz = lax.rem(z + dz, SIDE)
        pc = c if dc == 0 else 1 - c
        return pz, pc

    g_in = pltpu.make_async_copy(grad, gv, in_sem.at[0])
    h_in = pltpu.make_async_copy(hid, hv, in_sem.at[1])
    g_in.start()
    h_in.start()

    barrier = pltpu.get_barrier_semaphore()
    peers = []
    for dz, dc in zsteps:
        pz, pc = z_peer(dz, dc)
        peers.append((dp, pz * 2 + pc))
    for d in (1, 2, 3):
        peers.append(gather_peer(d))
    for d in (1, 3):
        peers.append(sum_peer(d))
    for peer in peers:
        pl.semaphore_signal(barrier, inc=1, device_id=peer, device_id_type=MESH)

    pairs = 2 * tokens
    route = jnp.concatenate([routes[0:1, :], routes[1:2, :]], axis=1)
    gate = jnp.concatenate([gates[0:1, :], gates[1:2, :]], axis=1)
    local_id = (ids[0:1, :] - dp * EX_BLK).astype(F32)
    local_id = jnp.concatenate([local_id, local_id], axis=1)
    expert_of = lax.broadcasted_iota(jnp.int32, (EXPERTS, pairs), 0)
    chosen = route == expert_of
    before = lax.broadcasted_iota(jnp.int32, (pairs, pairs), 0) < lax.broadcasted_iota(
        jnp.int32, (pairs, pairs), 1
    )
    place = _dot(
        jnp.where(chosen, 1.0, 0.0).astype(BF16), jnp.where(before, 1.0, 0.0).astype(BF16)
    )
    base = (lax.rem(expert_of, 2) * half + lax.div(expert_of, 2) * cap).astype(F32)
    slot = jnp.sum(jnp.where(chosen, base + place, 0.0), axis=0, keepdims=True)
    hit = slot == lax.broadcasted_iota(jnp.int32, (rows, pairs), 0).astype(F32)
    hot = jnp.where(hit, 1.0, 0.0)
    token_hot = (hot[:, 0:tokens] + hot[:, tokens:]).astype(BF16)
    slot_gate = jnp.sum(jnp.where(hit, gate, 0.0), axis=1, keepdims=True)

    def pack_grads(first, last):
        for n in range(first // TILE, last // TILE):
            cols = slice(n * TILE, (n + 1) * TILE)
            gs[:, cols] = (slot_gate * _dot(token_hot, gv[:, cols])).astype(BF16)

    g_in.wait()
    pack_grads(*g_cols[0])
    pl.semaphore_wait(barrier, len(peers))

    my_rows = pl.ds(pl.multiple_of(ex * cap, 16), cap)
    my_grad_rows = pl.ds(pl.multiple_of(3 * rows + ex * cap, 16), cap)

    def block(pz, pc):
        return pl.ds(pl.multiple_of(pc * half + pz * cap, 16), cap)

    def z_copies(k):
        copies = []
        for i, (dz, dc) in enumerate(zsteps):
            pz, pc = z_peer(dz, dc)
            if k < 2:
                cols = slice(*g_cols[k])
                src, dst = gs.at[block(pz, pc), cols], gall.at[my_grad_rows, cols]
            else:
                src, dst = hs.at[k - 2, block(pz, pc)], hin.at[k - 2, my_rows]
            copies.append(
                pltpu.make_async_remote_copy(
                    src_ref=src,
                    dst_ref=dst,
                    send_sem=z_send.at[k, i],
                    recv_sem=z_recv.at[k, i],
                    device_id=(dp, pz * 2 + pc),
                    device_id_type=MESH,
                )
            )
        return copies

    zc = [z_copies(k) for k in range(2 + SIDE)]
    for copy in zc[0]:
        copy.start()

    pack_grads(*g_cols[1])
    slot_id = jnp.sum(jnp.where(hit, local_id + 1.0, 0.0), axis=1, keepdims=True) - 1.0
    lane = lax.broadcasted_iota(jnp.int32, (rows, LANES), 1).astype(F32)
    gs[:, out_width:] = jnp.where(slot_id == lane, 1.0, 0.0).astype(BF16)
    for copy in zc[1]:
        copy.start()
    gall[my_grad_rows, :] = gs[block(z, c), :]

    from_pair = lax.broadcasted_iota(jnp.int32, (pairs, pairs), 0)
    to_pair = lax.broadcasted_iota(jnp.int32, (pairs, pairs), 1)
    interleave = 2 * lax.rem(from_pair, tokens) + lax.div(from_pair, tokens) == to_pair
    oh[...] = _dot(
        hot.astype(BF16), jnp.where(interleave, 1.0, 0.0).astype(BF16)
    ).astype(BF16)

    h_in.wait()
    for j in range(SIDE):
        for a in range(SIDE // 2):
            first, second = (2 * a * SIDE + j) * chunk, ((2 * a + 1) * SIDE + j) * chunk
            pair = jnp.concatenate(
                [
                    hv[:, :, first : first + chunk].reshape(pairs, chunk),
                    hv[:, :, second : second + chunk].reshape(pairs, chunk),
                ],
                axis=1,
            )
            at = j * slice_w + 2 * a * chunk
            hp[:, at : at + 2 * chunk] = pair

    def pack(q):
        je = pl.ds(pl.multiple_of(lax.rem(y + 1 + q, SIDE) * slice_w, LANES), slice_w)
        jo = pl.ds(pl.multiple_of(lax.rem(x + 1 + q, SIDE) * slice_w, LANES), slice_w)
        hs[q, 0:half, :] = _dot(oh[0:half, :], hp[:, je]).astype(BF16)
        hs[q, half:rows, :] = _dot(
            oh[half:rows, :], hv[:, :, jo].reshape(pairs, slice_w)
        ).astype(BF16)

    def forward_grads(k, d):
        cols = slice(*g_cols[k])
        return pltpu.make_async_remote_copy(
            src_ref=gall.at[3 * rows : 4 * rows, cols],
            dst_ref=gall.at[(d - 1) * rows : d * rows, cols],
            send_sem=fg_send.at[k, d - 1],
            recv_sem=fg_recv.at[k, d - 1],
            device_id=gather_peer(d),
            device_id_type=MESH,
        )

    def forward_hidden(q):
        return pltpu.make_async_remote_copy(
            src_ref=hin.at[q],
            dst_ref=hg.at[q],
            send_sem=fh_send.at[q],
            recv_sem=fh_recv.at[q],
            device_id=gather_peer(q + 1),
            device_id_type=MESH,
        )

    fgs = [[forward_grads(k, d) for d in (1, 2, 3)] for k in range(2)]
    fhs = [forward_hidden(q) for q in range(SIDE - 1)]

    for k in range(2 + SIDE):
        q = k - 2
        if 1 <= k < 1 + SIDE:
            pack(q + 1)
            for copy in zc[k + 1]:
                copy.start()
            hin[q + 1, my_rows, :] = hs[q + 1, block(z, c), :]
        for copy in zc[k]:
            copy.wait_recv()
        if k < 2:
            for copy in fgs[k]:
                copy.start()
            if k == 1:
                g = gall[3 * rows : 4 * rows, 0:out_width]
                b = gall[3 * rows : 4 * rows, out_width:]
                mgram[...] = _dot_t(g, g) * _dot_t(b, b)
        else:
            if q < SIDE - 1:
                fhs[q].start()
            h = hin[q]
            gram = _dot_t(h, h)
            if q > 0:
                gram = gram + hgram[...]
            if q < SIDE - 1:
                hgram[...] = gram
            else:
                row_sums = jnp.sum(gram * mgram[...], axis=1, keepdims=True)
                member = gall[3 * rows : 4 * rows, out_width:].astype(F32)
                part = jnp.sum(row_sums * member, axis=0, keepdims=True)
                sq_send[...] = jnp.broadcast_to(part, (8, LANES))

    sq_copies = []
    for i, (dz, dc) in enumerate(zsteps):
        pz, pc = z_peer(dz, dc)
        sq_copies.append(
            pltpu.make_async_remote_copy(
                src_ref=sq_send,
                dst_ref=sq_recv.at[i],
                send_sem=sq_ssem.at[i],
                recv_sem=sq_rsem.at[i],
                device_id=(dp, pz * 2 + pc),
                device_id_type=MESH,
            )
        )
    for copy in sq_copies:
        copy.start()
    ht[:, 3 * rows : 4 * rows] = hin[SIDE - 1].T
    total = sq_send[...]
    for i, copy in enumerate(sq_copies):
        copy.wait_recv()
        total = total + sq_recv[i]
    norms = jnp.sqrt(total)
    norm_out[...] = norms[0:1, 0:EX_BLK] / threshold
    f_send[...] = jnp.minimum(1.0, threshold / norms)
    f_copies = []
    for d in (1, 2, 3):
        f_copies.append(
            pltpu.make_async_remote_copy(
                src_ref=f_send,
                dst_ref=f_recv.at[d - 1],
                send_sem=f_ssem.at[d - 1],
                recv_sem=f_rsem.at[d - 1],
                device_id=gather_peer(d),
                device_id_type=MESH,
            )
        )
    for copy in f_copies:
        copy.start()
    for q in range(SIDE - 1):
        fhs[q].wait_recv()
        ht[:, q * rows : (q + 1) * rows] = hg[q].T
    for copy in fgs[0] + fgs[1]:
        copy.wait_recv()
        copy.wait_send()
    for copy in f_copies:
        copy.wait_recv()
    for q in range(SIDE):
        span = slice(q * rows, (q + 1) * rows)
        factors = f_send[0:1, :] if q == SIDE - 1 else f_recv[q, 0:1, :]
        row_factor = jnp.sum(
            gall[span, out_width:].astype(F32) * factors, axis=1, keepdims=True
        )
        rowf[span, :] = jnp.broadcast_to(row_factor, (rows, LANES))

    def chunk_rows(d, lower, size):
        start = lax.rem(rpos + d, SIDE) * chunk + lower * hc
        return pl.ds(pl.multiple_of(start, 32), size)

    def tile_at(n):
        return pl.ds(pl.multiple_of(n * TILE, TILE), TILE)

    def rs_copy(slot_, n):
        src = (
            part_a.at[0:hc],
            part_b.at[0],
            part_c.at[0],
            part_a.at[hc:chunk],
            part_b.at[1],
            part_c.at[1],
        )[slot_]
        return pltpu.make_async_remote_copy(
            src_ref=src.at[:, tile_at(n)],
            dst_ref=part_in.at[slot_, :, tile_at(n)],
            send_sem=rs_send.at[slot_, n],
            recv_sem=rs_recv.at[slot_, n],
            device_id=sum_peer(1 if slot_ < 3 else 3),
            device_id_type=MESH,
        )

    tiles = out_width // TILE

    @pl.loop(0, tiles)
    def _(n):
        cols = tile_at(n)
        wide = jnp.concatenate([rowf[...]] * (TILE // LANES), axis=1)
        gall[:, cols] = (wide * gall[:, cols].astype(F32)).astype(BF16)
        part_a[:, cols] = _dot(ht[chunk_rows(2, 0, chunk), :], gall[:, cols]).astype(BF16)
        rs_copy(0, n).start()
        rs_copy(3, n).start()

    @pl.loop(0, tiles)
    def _(n):
        cols = tile_at(n)
        part_b[0, :, cols] = _dot(ht[chunk_rows(1, 1, hc), :], gall[:, cols]).astype(BF16)
        rs_copy(1, n).start()
        part_b[1, :, cols] = _dot(ht[chunk_rows(3, 0, hc), :], gall[:, cols]).astype(BF16)
        rs_copy(4, n).start()

    @pl.loop(0, tiles)
    def _(n):
        cols = tile_at(n)
        term = _dot(ht[chunk_rows(1, 0, hc), :], gall[:, cols])
        rs_copy(0, n).wait_recv()
        part_c[0, :, cols] = (term + part_in[0, :, cols].astype(F32)).astype(BF16)
        rs_copy(2, n).start()
        term = _dot(ht[chunk_rows(3, 1, hc), :], gall[:, cols])
        rs_copy(3, n).wait_recv()
        part_c[1, :, cols] = (term + part_in[3, :, cols].astype(F32)).astype(BF16)
        rs_copy(5, n).start()

    @pl.loop(0, tiles)
    def _(n):
        cols = tile_at(n)
        own[:, cols] = _dot(ht[chunk_rows(0, 0, chunk), :], gall[:, cols])

    scale = 1.0 / (EX_BLK * SIDE * SIDE)

    @pl.loop(0, tiles)
    def _(n):
        cols = tile_at(n)
        for slot_ in (1, 2, 4, 5):
            rs_copy(slot_, n).wait_recv()
        upper = own[0:hc, cols] + part_in[2, :, cols].astype(F32) + part_in[4, :, cols].astype(F32)
        lower = own[hc:chunk, cols] + part_in[1, :, cols].astype(F32) + part_in[5, :, cols].astype(F32)
        out[0:hc, cols] = (upper * scale).astype(BF16)
        out[hc:chunk, cols] = (lower * scale).astype(BF16)

    for copies in zc:
        for copy in copies:
            copy.wait_send()
    for copy in fhs + sq_copies + f_copies:
        copy.wait_send()

    @pl.loop(0, tiles)
    def _(n):
        for slot_ in range(6):
            rs_copy(slot_, n).wait_send()


def body(hidden, grad_out, gate_weights, routes, example_ids):
    tokens, _, width = hidden.shape
    out_width = grad_out.shape[1]
    rows = 3 * tokens
    slice_w = width // SIDE
    chunk = slice_w // SIDE
    hc = chunk // 2
    wide = out_width + LANES
    tiles = out_width // TILE
    vmem = pl.BlockSpec(memory_space=pltpu.VMEM)
    hbm = pl.BlockSpec(memory_space=pl.ANY)
    dma = pltpu.SemaphoreType.DMA
    update, norms = pl.pallas_call(
        kernel,
        out_shape=(
            pltpu.VMEM((chunk, out_width), BF16),
            pltpu.VMEM((1, EX_BLK), F32),
        ),
        in_specs=[vmem, vmem, vmem, hbm, hbm],
        out_specs=(vmem, vmem),
        scratch_shapes=[
            pltpu.VMEM((tokens, 2, width), BF16),
            pltpu.VMEM((2 * tokens, width), BF16),
            pltpu.VMEM((tokens, out_width), BF16),
            pltpu.VMEM((rows, wide), BF16),
            pltpu.VMEM((SIDE, rows, slice_w), BF16),
            pltpu.VMEM((SIDE * rows, wide), BF16),
            pltpu.VMEM((SIDE, rows, slice_w), BF16),
            pltpu.VMEM((SIDE - 1, rows, slice_w), BF16),
            pltpu.VMEM((slice_w, SIDE * rows), BF16),
            pltpu.VMEM((rows, 2 * tokens), BF16),
            pltpu.VMEM((rows, rows), F32),
            pltpu.VMEM((rows, rows), F32),
            pltpu.VMEM((SIDE * rows, LANES), F32),
            pltpu.VMEM((8, LANES), F32),
            pltpu.VMEM((EXPERTS - 1, 8, LANES), F32),
            pltpu.VMEM((8, LANES), F32),
            pltpu.VMEM((SIDE - 1, 8, LANES), F32),
            pltpu.VMEM((chunk, out_width), BF16),
            pltpu.VMEM((2, hc, out_width), BF16),
            pltpu.VMEM((2, hc, out_width), BF16),
            pltpu.VMEM((6, hc, out_width), BF16),
            pltpu.VMEM((chunk, out_width), F32),
            dma((2,)),
            dma((2 + SIDE, EXPERTS - 1)),
            dma((2 + SIDE, EXPERTS - 1)),
            dma((2, SIDE - 1)),
            dma((2, SIDE - 1)),
            dma((SIDE - 1,)),
            dma((SIDE - 1,)),
            dma((EXPERTS - 1,)),
            dma((EXPERTS - 1,)),
            dma((SIDE - 1,)),
            dma((SIDE - 1,)),
            dma((6, tiles)),
            dma((6, tiles)),
        ],
        compiler_params=pltpu.CompilerParams(
            collective_id=0, has_side_effects=True, vmem_limit_bytes=54 * 1024 * 1024
        ),
    )(routes.T, gate_weights.T, example_ids[None], hidden, grad_out)
    return update[None], norms.reshape(EX_BLK)


def solution(mesh):
    return jax.shard_map(
        body,
        mesh=mesh,
        in_specs=(
            P(("dp", "expert"), None, None),
            P(("dp", "expert"), None),
            P(("dp", "expert"), None),
            P(("dp", "expert"), None),
            P(("dp", "expert")),
        ),
        out_specs=(P("expert", "dp", None), P("dp")),
        check_vma=False,
    )
```

```python
import math

import jax
import jax.numpy as jnp
from jax import lax
from jax.experimental import pallas as pl
from jax.experimental.pallas import tpu as pltpu
from jax.sharding import PartitionSpec as P

MESH = pl.DeviceIdType.MESH
BF16, F32 = jnp.bfloat16, jnp.float32

SIDE = 4
EXPERTS = 8
EX_BLK = 8
LANES = 128
TILE = 256


def _dot(a, b):
    return lax.dot_general(a, b, (((1,), (0,)), ((), ())), preferred_element_type=F32)


def _dot_t(a, b):
    return lax.dot_general(a, b, (((1,), (1,)), ((), ())), preferred_element_type=F32)


def kernel(
    routes, gates, ids, hid, grad, out, norm_out,
    hv, hp, gv, gs, hs, gall, hin, hg, ht, oh, hgram, mgram, rowf,
    sq_send, sq_recv, part_a, part_b, part_c, part_in, own,
    in_sem, z_send, z_recv, fg_send, fg_recv, fh_send, fh_recv,
    sq_ssem, sq_rsem, rs_send, rs_recv,
):
    tokens, _, width = hid.shape
    out_width = grad.shape[1]
    cap = 3 * tokens // EXPERTS
    rows = EXPERTS * cap
    half = rows // 2
    slice_w = width // SIDE
    chunk = slice_w // SIDE
    hc = chunk // 2
    g_cols = ((0, out_width // 2), (out_width // 2, out_width + LANES))
    half_w = slice_w // 2
    order = [(0, 0), (2, 0), (1, 0), (0, 1), (2, 1), (1, 1), (3, 0), (3, 1)]
    n_pieces = 2 + len(order)
    threshold = math.sqrt(width * out_width * tokens * (0.43 + 0.01 * tokens))

    dp, ex = lax.axis_index("dp"), lax.axis_index("expert")
    x, y = lax.div(dp, SIDE), lax.rem(dp, SIDE)
    z, c = lax.div(ex, 2), lax.rem(ex, 2)
    gpos = y + c * (x - y)
    rpos = x + c * (y - x)

    def along(d, turned):
        a = x * SIDE + lax.rem(y + d, SIDE)
        b = lax.rem(x + d, SIDE) * SIDE + y
        return (a + turned * (b - a), ex)

    def gather_peer(d):
        return along(d, c)

    def sum_peer(d):
        return along(d, 1 - c)

    zsteps = [(2, 0), (2, 1), (1, 0), (3, 0), (1, 1), (3, 1), (0, 1)]

    def z_peer(dz, dc):
        pz = lax.rem(z + dz, SIDE)
        pc = c if dc == 0 else 1 - c
        return pz, pc

    g_in = pltpu.make_async_copy(grad, gv, in_sem.at[0])
    h_in = pltpu.make_async_copy(hid, hv, in_sem.at[1])
    g_in.start()
    h_in.start()

    barrier = pltpu.get_barrier_semaphore()
    peers = []
    for dz, dc in zsteps:
        pz, pc = z_peer(dz, dc)
        peers.append((dp, pz * 2 + pc))
    for d in (1, 2, 3):
        peers.append(gather_peer(d))
    for d in (1, 3):
        peers.append(sum_peer(d))
    for peer in peers:
        pl.semaphore_signal(barrier, inc=1, device_id=peer, device_id_type=MESH)

    pairs = 2 * tokens
    route = jnp.concatenate([routes[0:1, :], routes[1:2, :]], axis=1)
    gate = jnp.concatenate([gates[0:1, :], gates[1:2, :]], axis=1)
    local_id = (ids[0:1, :] - dp * EX_BLK).astype(F32)
    local_id = jnp.concatenate([local_id, local_id], axis=1)
    expert_of = lax.broadcasted_iota(jnp.int32, (EXPERTS, pairs), 0)
    chosen = route == expert_of
    before = lax.broadcasted_iota(jnp.int32, (pairs, pairs), 0) < lax.broadcasted_iota(
        jnp.int32, (pairs, pairs), 1
    )
    place = _dot(
        jnp.where(chosen, 1.0, 0.0).astype(BF16), jnp.where(before, 1.0, 0.0).astype(BF16)
    )
    base = (lax.rem(expert_of, 2) * half + lax.div(expert_of, 2) * cap).astype(F32)
    slot = jnp.sum(jnp.where(chosen, base + place, 0.0), axis=0, keepdims=True)
    hit = slot == lax.broadcasted_iota(jnp.int32, (rows, pairs), 0).astype(F32)
    hot = jnp.where(hit, 1.0, 0.0)
    token_hot = (hot[:, 0:tokens] + hot[:, tokens:]).astype(BF16)
    slot_gate = jnp.sum(jnp.where(hit, gate, 0.0), axis=1, keepdims=True)

    def pack_grads(first, last):
        for n in range(first // TILE, last // TILE):
            cols = slice(n * TILE, (n + 1) * TILE)
            gs[:, cols] = (slot_gate * _dot(token_hot, gv[:, cols])).astype(BF16)

    g_in.wait()
    pack_grads(*g_cols[0])
    pl.semaphore_wait(barrier, len(peers))

    my_rows = pl.ds(pl.multiple_of(ex * cap, 16), cap)
    my_grad_rows = pl.ds(pl.multiple_of(3 * rows + ex * cap, 16), cap)

    def block(pz, pc):
        return pl.ds(pl.multiple_of(pc * half + pz * cap, 16), cap)

    def z_copies(k):
        copies = []
        for i, (dz, dc) in enumerate(zsteps):
            pz, pc = z_peer(dz, dc)
            if k < 2:
                cols = slice(*g_cols[k])
                src, dst = gs.at[block(pz, pc), cols], gall.at[my_grad_rows, cols]
            else:
                at = order[k - 2]
                src, dst = hs.at[(*at, block(pz, pc))], hin.at[(*at, my_rows)]
            copies.append(
                pltpu.make_async_remote_copy(
                    src_ref=src,
                    dst_ref=dst,
                    send_sem=z_send.at[k, i],
                    recv_sem=z_recv.at[k, i],
                    device_id=(dp, pz * 2 + pc),
                    device_id_type=MESH,
                )
            )
        return copies

    zc = [z_copies(k) for k in range(n_pieces)]
    for copy in zc[0]:
        copy.start()

    pack_grads(*g_cols[1])
    slot_id = jnp.sum(jnp.where(hit, local_id + 1.0, 0.0), axis=1, keepdims=True) - 1.0
    lane = lax.broadcasted_iota(jnp.int32, (rows, LANES), 1).astype(F32)
    gs[:, out_width:] = jnp.where(slot_id == lane, 1.0, 0.0).astype(BF16)
    for copy in zc[1]:
        copy.start()
    gall[my_grad_rows, :] = gs[block(z, c), :]

    from_pair = lax.broadcasted_iota(jnp.int32, (pairs, pairs), 0)
    to_pair = lax.broadcasted_iota(jnp.int32, (pairs, pairs), 1)
    interleave = 2 * lax.rem(from_pair, tokens) + lax.div(from_pair, tokens) == to_pair
    oh[...] = _dot(
        hot.astype(BF16), jnp.where(interleave, 1.0, 0.0).astype(BF16)
    ).astype(BF16)

    h_in.wait()
    for j in range(SIDE):
        for a in range(SIDE // 2):
            first, second = (2 * a * SIDE + j) * chunk, ((2 * a + 1) * SIDE + j) * chunk
            pair = jnp.concatenate(
                [
                    hv[:, :, first : first + chunk].reshape(pairs, chunk),
                    hv[:, :, second : second + chunk].reshape(pairs, chunk),
                ],
                axis=1,
            )
            at = j * slice_w + 2 * a * chunk
            hp[:, at : at + 2 * chunk] = pair

    def pack(q, h):
        je = lax.rem(y + 1 + q, SIDE) * slice_w + h * half_w
        jo = lax.rem(x + 1 + q, SIDE) * slice_w + h * half_w
        je, jo = (pl.ds(pl.multiple_of(j, LANES), half_w) for j in (je, jo))
        hs[q, h, 0:half, :] = _dot(oh[0:half, :], hp[:, je]).astype(BF16)
        hs[q, h, half:rows, :] = _dot(
            oh[half:rows, :], hv[:, :, jo].reshape(pairs, half_w)
        ).astype(BF16)

    def forward_grads(k, d):
        cols = slice(*g_cols[k])
        return pltpu.make_async_remote_copy(
            src_ref=gall.at[3 * rows : 4 * rows, cols],
            dst_ref=gall.at[(d - 1) * rows : d * rows, cols],
            send_sem=fg_send.at[k, d - 1],
            recv_sem=fg_recv.at[k, d - 1],
            device_id=gather_peer(d),
            device_id_type=MESH,
        )

    def forward_hidden(q, h):
        return pltpu.make_async_remote_copy(
            src_ref=hin.at[q, h],
            dst_ref=hg.at[q, h],
            send_sem=fh_send.at[q, h],
            recv_sem=fh_recv.at[q, h],
            device_id=gather_peer(q + 1),
            device_id_type=MESH,
        )

    fgs = [[forward_grads(k, d) for d in (1, 2, 3)] for k in range(2)]
    fhs = [[forward_hidden(q, h) for h in range(2)] for q in range(SIDE - 1)]

    def transpose(q, h, rows_in):
        ht[h * half_w : (h + 1) * half_w, q * rows : (q + 1) * rows] = rows_in.T

    def take(q, h):
        fhs[q][h].wait_recv()
        transpose(q, h, hg[q, h])

    takes = {6: [(0, 0)], 7: [(2, 0), (1, 0)], 8: [(0, 1), (2, 1)]}
    for k in range(n_pieces):
        if 1 <= k < n_pieces - 1:
            at = order[k - 1]
            pack(*at)
            for copy in zc[k + 1]:
                copy.start()
            hin[(*at, my_rows)] = hs[(*at, block(z, c))]
        for copy in zc[k]:
            copy.wait_recv()
        if k < 2:
            for copy in fgs[k]:
                copy.start()
            if k == 1:
                g = gall[3 * rows : 4 * rows, 0:out_width]
                b = gall[3 * rows : 4 * rows, out_width:]
                mgram[...] = _dot_t(g, g) * _dot_t(b, b)
        else:
            q, h = order[k - 2]
            if q < SIDE - 1:
                fhs[q][h].start()
            part = hin[q, h]
            gram = _dot_t(part, part)
            if k > 2:
                gram = gram + hgram[...]
            if k + 1 < n_pieces:
                hgram[...] = gram
            else:
                row_sums = jnp.sum(gram * mgram[...], axis=1, keepdims=True)
                member = gall[3 * rows : 4 * rows, out_width:].astype(F32)
                part = jnp.sum(row_sums * member, axis=0, keepdims=True)
                sq_send[...] = jnp.broadcast_to(part, (8, LANES))
            if q == SIDE - 1 and h == 0:
                transpose(q, h, hin[q, h])
            for at in takes.get(k, []):
                take(*at)

    sq_copies = []
    for d in (2, 1, 3, 0):
        for i, (dz, dc) in enumerate(zsteps + [(0, 0)]):
            if (d, dz, dc) == (0, 0, 0):
                continue
            pz, pc = z_peer(dz, dc)
            sq_copies.append(
                pltpu.make_async_remote_copy(
                    src_ref=sq_send,
                    dst_ref=sq_recv.at[d, i],
                    send_sem=sq_ssem.at[d, i],
                    recv_sem=sq_rsem.at[d, i],
                    device_id=(along(d, pc)[0], pz * 2 + pc),
                    device_id_type=MESH,
                )
            )
    for copy in sq_copies:
        copy.start()
    transpose(3, 1, hin[SIDE - 1, 1])
    take(1, 1)
    for copy in fgs[0] + fgs[1]:
        copy.wait_recv()
        copy.wait_send()
    for copy in sq_copies:
        copy.wait_recv()
    for q in range(SIDE):
        d = (q + 1) % SIDE
        total = sq_send[...] if d == 0 else sq_recv[d, EXPERTS - 1]
        for i in range(EXPERTS - 1):
            total = total + sq_recv[d, i]
        norms = jnp.sqrt(total)
        if d == 0:
            norm_out[...] = norms[0:1, 0:EX_BLK] / threshold
        factors = jnp.minimum(1.0, threshold / norms)[0:1, :]
        span = slice(q * rows, (q + 1) * rows)
        row_factor = jnp.sum(
            gall[span, out_width:].astype(F32) * factors, axis=1, keepdims=True
        )
        rowf[span, :] = jnp.broadcast_to(row_factor, (rows, LANES))

    def chunk_rows(d, lower, size):
        start = lax.rem(rpos + d, SIDE) * chunk + lower * hc
        return pl.ds(pl.multiple_of(start, 32), size)

    def tile_at(n):
        return pl.ds(pl.multiple_of(n * TILE, TILE), TILE)

    def rs_copy(slot_, n):
        src = (
            part_a.at[n, 0:hc],
            part_b.at[0, n],
            part_c.at[0, n],
            part_a.at[n, hc:chunk],
            part_b.at[1, n],
            part_c.at[1, n],
        )[slot_]
        return pltpu.make_async_remote_copy(
            src_ref=src,
            dst_ref=part_in.at[slot_, n],
            send_sem=rs_send.at[slot_, n],
            recv_sem=rs_recv.at[slot_, n],
            device_id=sum_peer(1 if slot_ < 3 else 3),
            device_id_type=MESH,
        )

    tiles = out_width // TILE

    @pl.loop(0, tiles)
    def _(n):
        cols = tile_at(n)
        wide = jnp.concatenate([rowf[...]] * (TILE // LANES), axis=1)
        gall[:, cols] = (wide * gall[:, cols].astype(F32)).astype(BF16)
        part_a[n] = _dot(ht[chunk_rows(2, 0, chunk), :], gall[:, cols]).astype(BF16)
        rs_copy(0, n).start()
        rs_copy(3, n).start()

    @pl.loop(0, tiles)
    def _(n):
        cols = tile_at(n)
        part_b[0, n] = _dot(ht[chunk_rows(1, 1, hc), :], gall[:, cols]).astype(BF16)
        rs_copy(1, n).start()
        part_b[1, n] = _dot(ht[chunk_rows(3, 0, hc), :], gall[:, cols]).astype(BF16)
        rs_copy(4, n).start()

    @pl.loop(0, tiles)
    def _(n):
        cols = tile_at(n)
        term = _dot(ht[chunk_rows(1, 0, hc), :], gall[:, cols])
        rs_copy(0, n).wait_recv()
        part_c[0, n] = (term + part_in[0, n].astype(F32)).astype(BF16)
        rs_copy(2, n).start()
        term = _dot(ht[chunk_rows(3, 1, hc), :], gall[:, cols])
        rs_copy(3, n).wait_recv()
        part_c[1, n] = (term + part_in[3, n].astype(F32)).astype(BF16)
        rs_copy(5, n).start()

    @pl.loop(0, tiles)
    def _(n):
        cols = tile_at(n)
        own[:, cols] = _dot(ht[chunk_rows(0, 0, chunk), :], gall[:, cols])

    scale = 1.0 / (EX_BLK * SIDE * SIDE)

    @pl.loop(0, tiles)
    def _(n):
        cols = tile_at(n)
        for slot_ in (1, 2, 4, 5):
            rs_copy(slot_, n).wait_recv()
        upper = own[0:hc, cols] + part_in[2, n].astype(F32) + part_in[4, n].astype(F32)
        lower = own[hc:chunk, cols] + part_in[1, n].astype(F32) + part_in[5, n].astype(F32)
        out[0:hc, cols] = (upper * scale).astype(BF16)
        out[hc:chunk, cols] = (lower * scale).astype(BF16)

    for copies in zc:
        for copy in copies:
            copy.wait_send()
    for copy in fhs[0] + fhs[1] + fhs[2] + sq_copies:
        copy.wait_send()

    @pl.loop(0, tiles)
    def _(n):
        for slot_ in range(6):
            rs_copy(slot_, n).wait_send()


def body(hidden, grad_out, gate_weights, routes, example_ids):
    tokens, _, width = hidden.shape
    out_width = grad_out.shape[1]
    rows = 3 * tokens
    slice_w = width // SIDE
    chunk = slice_w // SIDE
    hc = chunk // 2
    wide = out_width + LANES
    tiles = out_width // TILE
    vmem = pl.BlockSpec(memory_space=pltpu.VMEM)
    hbm = pl.BlockSpec(memory_space=pl.ANY)
    dma = pltpu.SemaphoreType.DMA
    update, norms = pl.pallas_call(
        kernel,
        out_shape=(
            pltpu.VMEM((chunk, out_width), BF16),
            pltpu.VMEM((1, EX_BLK), F32),
        ),
        in_specs=[vmem, vmem, vmem, hbm, hbm],
        out_specs=(vmem, vmem),
        scratch_shapes=[
            pltpu.VMEM((tokens, 2, width), BF16),
            pltpu.VMEM((2 * tokens, width), BF16),
            pltpu.VMEM((tokens, out_width), BF16),
            pltpu.VMEM((rows, wide), BF16),
            pltpu.VMEM((SIDE, 2, rows, slice_w // 2), BF16),
            pltpu.VMEM((SIDE * rows, wide), BF16),
            pltpu.VMEM((SIDE, 2, rows, slice_w // 2), BF16),
            pltpu.VMEM((SIDE - 1, 2, rows, slice_w // 2), BF16),
            pltpu.VMEM((slice_w, SIDE * rows), BF16),
            pltpu.VMEM((rows, 2 * tokens), BF16),
            pltpu.VMEM((rows, rows), F32),
            pltpu.VMEM((rows, rows), F32),
            pltpu.VMEM((SIDE * rows, LANES), F32),
            pltpu.VMEM((8, LANES), F32),
            pltpu.VMEM((SIDE, EXPERTS, 8, LANES), F32),
            pltpu.VMEM((tiles, chunk, TILE), BF16),
            pltpu.VMEM((2, tiles, hc, TILE), BF16),
            pltpu.VMEM((2, tiles, hc, TILE), BF16),
            pltpu.VMEM((6, tiles, hc, TILE), BF16),
            pltpu.VMEM((chunk, out_width), F32),
            dma((2,)),
            dma((2 + 2 * SIDE, EXPERTS - 1)),
            dma((2 + 2 * SIDE, EXPERTS - 1)),
            dma((2, SIDE - 1)),
            dma((2, SIDE - 1)),
            dma((SIDE - 1, 2)),
            dma((SIDE - 1, 2)),
            dma((SIDE, EXPERTS)),
            dma((SIDE, EXPERTS)),
            dma((6, tiles)),
            dma((6, tiles)),
        ],
        compiler_params=pltpu.CompilerParams(
            collective_id=0, has_side_effects=True, vmem_limit_bytes=55 * 1024 * 1024
        ),
    )(routes.T, gate_weights.T, example_ids[None], hidden, grad_out)
    return update[None], norms.reshape(EX_BLK)


def solution(mesh):
    return jax.shard_map(
        body,
        mesh=mesh,
        in_specs=(
            P(("dp", "expert"), None, None),
            P(("dp", "expert"), None),
            P(("dp", "expert"), None),
            P(("dp", "expert"), None),
            P(("dp", "expert")),
        ),
        out_specs=(P("expert", "dp", None), P("dp")),
        check_vma=False,
    )
```

```python
import math

import jax
import jax.numpy as jnp
from jax import lax
from jax.experimental import pallas as pl
from jax.experimental.pallas import tpu as pltpu
from jax.sharding import PartitionSpec as P

MESH = pl.DeviceIdType.MESH
BF16, F32 = jnp.bfloat16, jnp.float32

SIDE = 4
EXPERTS = 8
EX_BLK = 8
LANES = 128
TILE = 256


def _dot(a, b):
    return lax.dot_general(a, b, (((1,), (0,)), ((), ())), preferred_element_type=F32)


def _dot_t(a, b):
    return lax.dot_general(a, b, (((1,), (1,)), ((), ())), preferred_element_type=F32)


def kernel(
    routes_hbm, gates_hbm, ids_hbm, hid, grad, out, norm_out,
    routes, gates, ids,
    hv, hp, gv, gs, hs, gall, hin, hg, ht, oh, hgram, mgram, rowf,
    id_send, id_recv, sq_send, sq_recv, part_a, part_b, part_c, part_in, own,
    in_sem, z_send, z_recv, fg_send, fg_recv, fh_send, fh_recv,
    id_ssem, id_rsem, sq_ssem, sq_rsem, rs_send, rs_recv,
):
    tokens, _, width = hid.shape
    out_width = grad.shape[1]
    cap = 3 * tokens // EXPERTS
    rows = EXPERTS * cap
    half = rows // 2
    slice_w = width // SIDE
    chunk = slice_w // SIDE
    hc = chunk // 2
    g_cols = ((0, out_width // 2), (out_width // 2, out_width))
    half_w = slice_w // 2
    order = [(0, 0), (2, 0), (1, 0), (0, 1), (2, 1), (1, 1), (3, 0), (3, 1)]
    n_pieces = 2 + len(order)
    threshold = math.sqrt(width * out_width * tokens * (0.43 + 0.01 * tokens))

    dp, ex = lax.axis_index("dp"), lax.axis_index("expert")
    x, y = lax.div(dp, SIDE), lax.rem(dp, SIDE)
    z, c = lax.div(ex, 2), lax.rem(ex, 2)
    gpos = y + c * (x - y)
    rpos = x + c * (y - x)

    def along(d, turned):
        a = x * SIDE + lax.rem(y + d, SIDE)
        b = lax.rem(x + d, SIDE) * SIDE + y
        return (a + turned * (b - a), ex)

    def gather_peer(d):
        return along(d, c)

    def sum_peer(d):
        return along(d, 1 - c)

    zsteps = [(2, 0), (2, 1), (1, 0), (3, 0), (1, 1), (3, 1), (0, 1)]

    def z_peer(dz, dc):
        pz = lax.rem(z + dz, SIDE)
        pc = c if dc == 0 else 1 - c
        return pz, pc

    barrier = pltpu.get_barrier_semaphore()
    peers = []
    for dz, dc in zsteps:
        pz, pc = z_peer(dz, dc)
        peers.append((dp, pz * 2 + pc))
    for d in (1, 2, 3):
        peers.append(gather_peer(d))
    for peer in peers:
        pl.semaphore_signal(barrier, inc=1, device_id=peer, device_id_type=MESH)
    small_in = [
        pltpu.make_async_copy(src, dst, in_sem.at[2 + i])
        for i, (src, dst) in enumerate(
            [(routes_hbm, routes), (gates_hbm, gates), (ids_hbm, ids)]
        )
    ]
    g_in = pltpu.make_async_copy(grad, gv, in_sem.at[0])
    h_in = pltpu.make_async_copy(hid, hv, in_sem.at[1])
    for copy in small_in + [g_in, h_in]:
        copy.start()
    for copy in small_in:
        copy.wait()

    pairs = 2 * tokens
    route = jnp.concatenate([routes[0:1, :], routes[1:2, :]], axis=1)
    gate = jnp.concatenate([gates[0:1, :], gates[1:2, :]], axis=1)
    local_id = (ids[0:1, :] - dp * EX_BLK).astype(F32)
    local_id = jnp.concatenate([local_id, local_id], axis=1)
    expert_of = lax.broadcasted_iota(jnp.int32, (EXPERTS, pairs), 0)
    chosen = route == expert_of
    before = lax.broadcasted_iota(jnp.int32, (pairs, pairs), 0) < lax.broadcasted_iota(
        jnp.int32, (pairs, pairs), 1
    )
    place = _dot(
        jnp.where(chosen, 1.0, 0.0).astype(BF16), jnp.where(before, 1.0, 0.0).astype(BF16)
    )
    base = (lax.rem(expert_of, 2) * half + lax.div(expert_of, 2) * cap).astype(F32)
    slot = jnp.sum(jnp.where(chosen, base + place, 0.0), axis=0, keepdims=True)
    hit = slot == lax.broadcasted_iota(jnp.int32, (rows, pairs), 0).astype(F32)
    hot = jnp.where(hit, 1.0, 0.0)
    token_hot = (hot[:, 0:tokens] + hot[:, tokens:]).astype(BF16)
    slot_gate = jnp.sum(jnp.where(hit, gate, 0.0), axis=1, keepdims=True)
    hot16 = hot.astype(BF16)
    slot_id = _dot_t(jnp.broadcast_to(local_id + 1.0, (8, pairs)).astype(BF16), hot16)[0:1, :]
    for j in range(EXPERTS):
        id_send[j] = jnp.concatenate(
            [slot_id[:, j * cap : (j + 1) * cap], jnp.zeros((1, LANES - cap), F32)], axis=1
        )

    def pack_grads(first, last):
        for n in range(first // TILE, last // TILE):
            cols = slice(n * TILE, (n + 1) * TILE)
            gs[:, cols] = (slot_gate * _dot(token_hot, gv[:, cols])).astype(BF16)

    g_in.wait()
    pack_grads(*g_cols[0])
    pl.semaphore_wait(barrier, len(peers))

    my_rows = pl.ds(pl.multiple_of(ex * cap, 16), cap)
    my_grad_rows = pl.ds(pl.multiple_of(3 * rows + ex * cap, 16), cap)

    def block(pz, pc):
        return pl.ds(pl.multiple_of(pc * half + pz * cap, 16), cap)

    def z_copies(k):
        copies = []
        for i, (dz, dc) in enumerate(zsteps):
            pz, pc = z_peer(dz, dc)
            if k < 2:
                cols = slice(*g_cols[k])
                src, dst = gs.at[block(pz, pc), cols], gall.at[my_grad_rows, cols]
            else:
                at = order[k - 2]
                src, dst = hs.at[(*at, block(pz, pc))], hin.at[(*at, my_rows)]
            copies.append(
                pltpu.make_async_remote_copy(
                    src_ref=src,
                    dst_ref=dst,
                    send_sem=z_send.at[k, i],
                    recv_sem=z_recv.at[k, i],
                    device_id=(dp, pz * 2 + pc),
                    device_id_type=MESH,
                )
            )
        return copies

    id_copies = []
    for i, (dz, dc) in enumerate(zsteps):
        pz, pc = z_peer(dz, dc)
        id_copies.append(
            pltpu.make_async_remote_copy(
                src_ref=id_send.at[pc * SIDE + pz],
                dst_ref=id_recv.at[ex],
                send_sem=id_ssem.at[i],
                recv_sem=id_rsem.at[i],
                device_id=(dp, pz * 2 + pc),
                device_id_type=MESH,
            )
        )
    zc = [z_copies(k) for k in range(n_pieces)]
    for copy in zc[0] + id_copies:
        copy.start()

    pack_grads(*g_cols[1])
    for copy in zc[1]:
        copy.start()
    gall[my_grad_rows, 0:out_width] = gs[block(z, c), :]
    id_recv[ex] = id_send[c * SIDE + z]

    from_pair = lax.broadcasted_iota(jnp.int32, (pairs, pairs), 0)
    to_pair = lax.broadcasted_iota(jnp.int32, (pairs, pairs), 1)
    interleave = 2 * lax.rem(from_pair, tokens) + lax.div(from_pair, tokens) == to_pair
    oh[...] = _dot(
        hot16, jnp.where(interleave, 1.0, 0.0).astype(BF16)
    ).astype(BF16)

    h_in.wait()
    for j in range(SIDE):
        for a in range(SIDE // 2):
            first, second = (2 * a * SIDE + j) * chunk, ((2 * a + 1) * SIDE + j) * chunk
            pair = jnp.concatenate(
                [
                    hv[:, :, first : first + chunk].reshape(pairs, chunk),
                    hv[:, :, second : second + chunk].reshape(pairs, chunk),
                ],
                axis=1,
            )
            at = j * slice_w + 2 * a * chunk
            hp[:, at : at + 2 * chunk] = pair

    def pack(q, h):
        je = lax.rem(y + 1 + q, SIDE) * slice_w + h * half_w
        jo = lax.rem(x + 1 + q, SIDE) * slice_w + h * half_w
        je, jo = (pl.ds(pl.multiple_of(j, LANES), half_w) for j in (je, jo))
        hs[q, h, 0:half, :] = _dot(oh[0:half, :], hp[:, je]).astype(BF16)
        hs[q, h, half:rows, :] = _dot(
            oh[half:rows, :], hv[:, :, jo].reshape(pairs, half_w)
        ).astype(BF16)

    def forward_grads(k, d):
        cols = slice(g_cols[k][0], g_cols[k][1] + k * LANES)
        return pltpu.make_async_remote_copy(
            src_ref=gall.at[3 * rows : 4 * rows, cols],
            dst_ref=gall.at[(d - 1) * rows : d * rows, cols],
            send_sem=fg_send.at[k, d - 1],
            recv_sem=fg_recv.at[k, d - 1],
            device_id=gather_peer(d),
            device_id_type=MESH,
        )

    def forward_hidden(q, h):
        return pltpu.make_async_remote_copy(
            src_ref=hin.at[q, h],
            dst_ref=hg.at[q, h],
            send_sem=fh_send.at[q, h],
            recv_sem=fh_recv.at[q, h],
            device_id=gather_peer(q + 1),
            device_id_type=MESH,
        )

    fgs = [[forward_grads(k, d) for d in (1, 2, 3)] for k in range(2)]
    fhs = [[forward_hidden(q, h) for h in range(2)] for q in range(SIDE - 1)]

    def transpose(q, h, rows_in):
        ht[h * half_w : (h + 1) * half_w, q * rows : (q + 1) * rows] = rows_in.T

    def take(q, h):
        fhs[q][h].wait_recv()
        transpose(q, h, hg[q, h])

    takes = {6: [(0, 0)], 7: [(2, 0), (1, 0)], 8: [(0, 1), (2, 1)]}
    for k in range(n_pieces):
        if 1 <= k < n_pieces - 1:
            at = order[k - 1]
            pack(*at)
            for copy in zc[k + 1]:
                copy.start()
            hin[(*at, my_rows)] = hs[(*at, block(z, c))]
        for copy in zc[k]:
            copy.wait_recv()
        if k == 1:
            for copy in id_copies:
                copy.wait_recv()
            ids_in = jnp.concatenate([id_recv[e][:, 0:cap] for e in range(EXPERTS)], axis=1)
            ids_in = jnp.broadcast_to(ids_in, (8, rows)).T[:, 0:1]
            lane = lax.broadcasted_iota(jnp.int32, (rows, LANES), 1).astype(F32) + 1.0
            gall[3 * rows : 4 * rows, out_width:] = jnp.where(ids_in == lane, 1.0, 0.0).astype(BF16)
        if k < 2:
            for copy in fgs[k]:
                copy.start()
            if k == 1:
                g = gall[3 * rows : 4 * rows, 0:out_width]
                b = gall[3 * rows : 4 * rows, out_width:]
                mgram[...] = _dot_t(g, g) * _dot_t(b, b)
        else:
            q, h = order[k - 2]
            if q < SIDE - 1:
                fhs[q][h].start()
            part = hin[q, h]
            gram = _dot_t(part, part)
            if k > 2:
                gram = gram + hgram[...]
            if k + 1 < n_pieces:
                hgram[...] = gram
            else:
                row_sums = jnp.sum(gram * mgram[...], axis=1, keepdims=True)
                member = gall[3 * rows : 4 * rows, out_width:].astype(F32)
                part = jnp.sum(row_sums * member, axis=0, keepdims=True)
                sq_send[...] = jnp.broadcast_to(part, (8, LANES))
            if q == SIDE - 1 and h == 0:
                transpose(q, h, hin[q, h])
            for at in takes.get(k, []):
                take(*at)

    sq_copies = []
    for d in (2, 1, 3, 0):
        for i, (dz, dc) in enumerate(zsteps + [(0, 0)]):
            if (d, dz, dc) == (0, 0, 0):
                continue
            pz, pc = z_peer(dz, dc)
            sq_copies.append(
                pltpu.make_async_remote_copy(
                    src_ref=sq_send,
                    dst_ref=sq_recv.at[d, i],
                    send_sem=sq_ssem.at[d, i],
                    recv_sem=sq_rsem.at[d, i],
                    device_id=(along(d, pc)[0], pz * 2 + pc),
                    device_id_type=MESH,
                )
            )
    for copy in sq_copies:
        copy.start()
    transpose(3, 1, hin[SIDE - 1, 1])
    take(1, 1)
    for copy in fgs[0] + fgs[1]:
        copy.wait_recv()
        copy.wait_send()
    for copy in sq_copies:
        copy.wait_recv()
    for q in range(SIDE):
        d = (q + 1) % SIDE
        total = sq_send[...] if d == 0 else sq_recv[d, EXPERTS - 1]
        for i in range(EXPERTS - 1):
            total = total + sq_recv[d, i]
        norms = jnp.sqrt(total)
        if d == 0:
            norm_out[...] = norms[0:1, 0:EX_BLK] / threshold
        factors = jnp.minimum(1.0, threshold / norms)[0:1, :]
        span = slice(q * rows, (q + 1) * rows)
        row_factor = jnp.sum(
            gall[span, out_width:].astype(F32) * factors, axis=1, keepdims=True
        )
        rowf[span, :] = jnp.broadcast_to(row_factor, (rows, LANES))

    def chunk_rows(d, lower, size):
        start = lax.rem(rpos + d, SIDE) * chunk + lower * hc
        return pl.ds(pl.multiple_of(start, 32), size)

    def tile_at(n):
        return pl.ds(pl.multiple_of(n * TILE, TILE), TILE)

    def rs_copy(slot_, n):
        src = (
            part_a.at[n, 0:hc],
            part_b.at[0, n],
            part_c.at[0, n],
            part_a.at[n, hc:chunk],
            part_b.at[1, n],
            part_c.at[1, n],
        )[slot_]
        return pltpu.make_async_remote_copy(
            src_ref=src,
            dst_ref=part_in.at[slot_, n],
            send_sem=rs_send.at[slot_, n],
            recv_sem=rs_recv.at[slot_, n],
            device_id=sum_peer(1 if slot_ < 3 else 3),
            device_id_type=MESH,
        )

    tiles = out_width // TILE

    @pl.loop(0, tiles)
    def _(n):
        cols = tile_at(n)
        wide = jnp.concatenate([rowf[...]] * (TILE // LANES), axis=1)
        gall[:, cols] = (wide * gall[:, cols].astype(F32)).astype(BF16)
        part_a[n] = _dot(ht[chunk_rows(2, 0, chunk), :], gall[:, cols]).astype(BF16)
        rs_copy(0, n).start()
        rs_copy(3, n).start()

    @pl.loop(0, tiles)
    def _(n):
        cols = tile_at(n)
        part_b[0, n] = _dot(ht[chunk_rows(1, 1, hc), :], gall[:, cols]).astype(BF16)
        rs_copy(1, n).start()
        part_b[1, n] = _dot(ht[chunk_rows(3, 0, hc), :], gall[:, cols]).astype(BF16)
        rs_copy(4, n).start()

    @pl.loop(0, tiles)
    def _(n):
        cols = tile_at(n)
        term = _dot(ht[chunk_rows(1, 0, hc), :], gall[:, cols])
        rs_copy(0, n).wait_recv()
        part_c[0, n] = (term + part_in[0, n].astype(F32)).astype(BF16)
        rs_copy(2, n).start()
        term = _dot(ht[chunk_rows(3, 1, hc), :], gall[:, cols])
        rs_copy(3, n).wait_recv()
        part_c[1, n] = (term + part_in[3, n].astype(F32)).astype(BF16)
        rs_copy(5, n).start()

    @pl.loop(0, tiles)
    def _(n):
        cols = tile_at(n)
        own[:, cols] = _dot(ht[chunk_rows(0, 0, chunk), :], gall[:, cols])

    scale = 1.0 / (EX_BLK * SIDE * SIDE)

    @pl.loop(0, tiles)
    def _(n):
        cols = tile_at(n)
        for slot_ in (1, 2, 4, 5):
            rs_copy(slot_, n).wait_recv()
        upper = own[0:hc, cols] + part_in[2, n].astype(F32) + part_in[4, n].astype(F32)
        lower = own[hc:chunk, cols] + part_in[1, n].astype(F32) + part_in[5, n].astype(F32)
        out[0:hc, cols] = (upper * scale).astype(BF16)
        out[hc:chunk, cols] = (lower * scale).astype(BF16)

    for copies in zc + [id_copies]:
        for copy in copies:
            copy.wait_send()
    for copy in fhs[0] + fhs[1] + fhs[2] + sq_copies:
        copy.wait_send()

    @pl.loop(0, tiles)
    def _(n):
        for slot_ in range(6):
            rs_copy(slot_, n).wait_send()


def body(hidden, grad_out, gate_weights, routes, example_ids):
    tokens, _, width = hidden.shape
    out_width = grad_out.shape[1]
    rows = 3 * tokens
    slice_w = width // SIDE
    chunk = slice_w // SIDE
    hc = chunk // 2
    wide = out_width + LANES
    tiles = out_width // TILE
    vmem = pl.BlockSpec(memory_space=pltpu.VMEM)
    hbm = pl.BlockSpec(memory_space=pl.ANY)
    dma = pltpu.SemaphoreType.DMA
    update, norms = pl.pallas_call(
        kernel,
        out_shape=(
            pltpu.VMEM((chunk, out_width), BF16),
            pltpu.VMEM((1, EX_BLK), F32),
        ),
        in_specs=[hbm] * 5,
        out_specs=(vmem, vmem),
        scratch_shapes=[
            pltpu.VMEM((2, tokens), jnp.int32),
            pltpu.VMEM((2, tokens), F32),
            pltpu.VMEM((1, tokens), jnp.int32),
            pltpu.VMEM((tokens, 2, width), BF16),
            pltpu.VMEM((2 * tokens, width), BF16),
            pltpu.VMEM((tokens, out_width), BF16),
            pltpu.VMEM((rows, out_width), BF16),
            pltpu.VMEM((SIDE, 2, rows, slice_w // 2), BF16),
            pltpu.VMEM((SIDE * rows, wide), BF16),
            pltpu.VMEM((SIDE, 2, rows, slice_w // 2), BF16),
            pltpu.VMEM((SIDE - 1, 2, rows, slice_w // 2), BF16),
            pltpu.VMEM((slice_w, SIDE * rows), BF16),
            pltpu.VMEM((rows, 2 * tokens), BF16),
            pltpu.VMEM((rows, rows), F32),
            pltpu.VMEM((rows, rows), F32),
            pltpu.VMEM((SIDE * rows, LANES), F32),
            pltpu.VMEM((EXPERTS, 1, LANES), F32),
            pltpu.VMEM((EXPERTS, 1, LANES), F32),
            pltpu.VMEM((8, LANES), F32),
            pltpu.VMEM((SIDE, EXPERTS, 8, LANES), F32),
            pltpu.VMEM((tiles, chunk, TILE), BF16),
            pltpu.VMEM((2, tiles, hc, TILE), BF16),
            pltpu.VMEM((2, tiles, hc, TILE), BF16),
            pltpu.VMEM((6, tiles, hc, TILE), BF16),
            pltpu.VMEM((chunk, out_width), F32),
            dma((5,)),
            dma((2 + 2 * SIDE, EXPERTS - 1)),
            dma((2 + 2 * SIDE, EXPERTS - 1)),
            dma((2, SIDE - 1)),
            dma((2, SIDE - 1)),
            dma((SIDE - 1, 2)),
            dma((SIDE - 1, 2)),
            dma((EXPERTS - 1,)),
            dma((EXPERTS - 1,)),
            dma((SIDE, EXPERTS)),
            dma((SIDE, EXPERTS)),
            dma((6, tiles)),
            dma((6, tiles)),
        ],
        compiler_params=pltpu.CompilerParams(
            collective_id=0, has_side_effects=True, vmem_limit_bytes=55 * 1024 * 1024
        ),
    )(routes.T, gate_weights.T, example_ids[None], hidden, grad_out)
    return update[None], norms.reshape(EX_BLK)


def solution(mesh):
    return jax.shard_map(
        body,
        mesh=mesh,
        in_specs=(
            P(("dp", "expert"), None, None),
            P(("dp", "expert"), None),
            P(("dp", "expert"), None),
            P(("dp", "expert"), None),
            P(("dp", "expert")),
        ),
        out_specs=(P("expert", "dp", None), P("dp")),
        check_vma=False,
    )
```

```python
import math

import jax
import jax.numpy as jnp
from jax import lax
from jax.experimental import pallas as pl
from jax.experimental.pallas import tpu as pltpu
from jax.sharding import PartitionSpec as P

MESH = pl.DeviceIdType.MESH
BF16, F32 = jnp.bfloat16, jnp.float32

SIDE = 4
EXPERTS = 8
EX_BLK = 8
LANES = 128
TILE = 256


def _dot(a, b):
    return lax.dot_general(a, b, (((1,), (0,)), ((), ())), preferred_element_type=F32)


def _dot_t(a, b):
    return lax.dot_general(a, b, (((1,), (1,)), ((), ())), preferred_element_type=F32)


def kernel(
    routes_hbm, gates_hbm, ids_hbm, hid, grad, out, norm_out,
    routes, gates, ids,
    hv, hp, gv, gs, hs, gall, hin, hg, ht, oh, hgram, mgram, rowf,
    id_send, id_recv, sq_send, sq_recv, part_a, part_b, part_c, part_in, own,
    in_sem, z_send, z_recv, fg_send, fg_recv, fh_send, fh_recv,
    id_ssem, id_rsem, sq_ssem, sq_rsem, rs_send, rs_recv,
):
    tokens, _, width = hid.shape
    out_width = grad.shape[1]
    cap = 3 * tokens // EXPERTS
    rows = EXPERTS * cap
    half = rows // 2
    slice_w = width // SIDE
    chunk = slice_w // SIDE
    hc = chunk // 2
    g_cols = ((0, out_width // 2), (out_width // 2, out_width))
    half_w = slice_w // 2
    order = [(0, 0), (2, 0), (1, 0), (0, 1), (2, 1), (1, 1), (3, 0), (3, 1)]
    n_pieces = 2 + len(order)
    threshold = math.sqrt(width * out_width * tokens * (0.43 + 0.01 * tokens))

    dp, ex = lax.axis_index("dp"), lax.axis_index("expert")
    x, y = lax.div(dp, SIDE), lax.rem(dp, SIDE)
    z, c = lax.div(ex, 2), lax.rem(ex, 2)
    gpos = y + c * (x - y)
    rpos = x + c * (y - x)

    def along(d, turned):
        a = x * SIDE + lax.rem(y + d, SIDE)
        b = lax.rem(x + d, SIDE) * SIDE + y
        return (a + turned * (b - a), ex)

    def gather_peer(d):
        return along(d, c)

    def sum_peer(d):
        return along(d, 1 - c)

    zsteps = [(2, 0), (2, 1), (1, 0), (3, 0), (1, 1), (3, 1), (0, 1)]

    def z_peer(dz, dc):
        pz = lax.rem(z + dz, SIDE)
        pc = c if dc == 0 else 1 - c
        return pz, pc

    barrier = pltpu.get_barrier_semaphore()
    peers = []
    for dz, dc in zsteps:
        pz, pc = z_peer(dz, dc)
        peers.append((dp, pz * 2 + pc))
    for d in (1, 2, 3):
        peers.append(gather_peer(d))
    for peer in peers:
        pl.semaphore_signal(barrier, inc=1, device_id=peer, device_id_type=MESH)
    small_in = [
        pltpu.make_async_copy(src, dst, in_sem.at[2 + i])
        for i, (src, dst) in enumerate(
            [(routes_hbm, routes), (gates_hbm, gates), (ids_hbm, ids)]
        )
    ]
    g_in = pltpu.make_async_copy(grad, gv, in_sem.at[0])
    h_in = pltpu.make_async_copy(hid, hv, in_sem.at[1])
    for copy in small_in + [g_in, h_in]:
        copy.start()
    for copy in small_in:
        copy.wait()

    pairs = 2 * tokens
    route = jnp.concatenate([routes[0:1, :], routes[1:2, :]], axis=1)
    gate = jnp.concatenate([gates[0:1, :], gates[1:2, :]], axis=1)
    local_id = (ids[0:1, :] - dp * EX_BLK).astype(F32)
    local_id = jnp.concatenate([local_id, local_id], axis=1)
    expert_of = lax.broadcasted_iota(jnp.int32, (EXPERTS, pairs), 0)
    chosen = route == expert_of
    before = lax.broadcasted_iota(jnp.int32, (pairs, pairs), 0) < lax.broadcasted_iota(
        jnp.int32, (pairs, pairs), 1
    )
    place = _dot(
        jnp.where(chosen, 1.0, 0.0).astype(BF16), jnp.where(before, 1.0, 0.0).astype(BF16)
    )
    base = (lax.rem(expert_of, 2) * half + lax.div(expert_of, 2) * cap).astype(F32)
    slot = jnp.sum(jnp.where(chosen, base + place, 0.0), axis=0, keepdims=True)
    hit = slot == lax.broadcasted_iota(jnp.int32, (rows, pairs), 0).astype(F32)
    hot = jnp.where(hit, 1.0, 0.0)
    token_hot = (hot[:, 0:tokens] + hot[:, tokens:]).astype(BF16)
    slot_gate = jnp.sum(jnp.where(hit, gate, 0.0), axis=1, keepdims=True)
    hot16 = hot.astype(BF16)
    slot_id = _dot_t(jnp.broadcast_to(local_id + 1.0, (8, pairs)).astype(BF16), hot16)[0:1, :]
    for j in range(EXPERTS):
        id_send[j] = jnp.concatenate(
            [slot_id[:, j * cap : (j + 1) * cap], jnp.zeros((1, LANES - cap), F32)], axis=1
        )

    def pack_grads(first, last):
        for n in range(first // TILE, last // TILE):
            cols = slice(n * TILE, (n + 1) * TILE)
            gs[:, cols] = (slot_gate * _dot(token_hot, gv[:, cols])).astype(BF16)

    g_in.wait()
    pack_grads(*g_cols[0])
    pl.semaphore_wait(barrier, len(peers))

    my_rows = pl.ds(pl.multiple_of(ex * cap, 16), cap)
    my_grad_rows = pl.ds(pl.multiple_of(3 * rows + ex * cap, 16), cap)

    def block(pz, pc):
        return pl.ds(pl.multiple_of(pc * half + pz * cap, 16), cap)

    def z_copies(k):
        copies = []
        for i, (dz, dc) in enumerate(zsteps):
            pz, pc = z_peer(dz, dc)
            if k < 2:
                cols = slice(*g_cols[k])
                src, dst = gs.at[block(pz, pc), cols], gall.at[my_grad_rows, cols]
            else:
                at = order[k - 2]
                src, dst = hs.at[(*at, block(pz, pc))], hin.at[(*at, my_rows)]
            copies.append(
                pltpu.make_async_remote_copy(
                    src_ref=src,
                    dst_ref=dst,
                    send_sem=z_send.at[k, i],
                    recv_sem=z_recv.at[k, i],
                    device_id=(dp, pz * 2 + pc),
                    device_id_type=MESH,
                )
            )
        return copies

    id_copies = []
    for i, (dz, dc) in enumerate(zsteps):
        pz, pc = z_peer(dz, dc)
        id_copies.append(
            pltpu.make_async_remote_copy(
                src_ref=id_send.at[pc * SIDE + pz],
                dst_ref=id_recv.at[ex],
                send_sem=id_ssem.at[i],
                recv_sem=id_rsem.at[i],
                device_id=(dp, pz * 2 + pc),
                device_id_type=MESH,
            )
        )
    zc = [z_copies(k) for k in range(n_pieces)]
    for copy in zc[0] + id_copies:
        copy.start()

    pack_grads(*g_cols[1])
    for copy in zc[1]:
        copy.start()
    gall[my_grad_rows, 0:out_width] = gs[block(z, c), :]
    id_recv[ex] = id_send[c * SIDE + z]

    from_pair = lax.broadcasted_iota(jnp.int32, (pairs, pairs), 0)
    to_pair = lax.broadcasted_iota(jnp.int32, (pairs, pairs), 1)
    interleave = 2 * lax.rem(from_pair, tokens) + lax.div(from_pair, tokens) == to_pair
    oh[...] = _dot(
        hot16, jnp.where(interleave, 1.0, 0.0).astype(BF16)
    ).astype(BF16)

    h_in.wait()
    for j in range(SIDE):
        for a in range(SIDE // 2):
            first, second = (2 * a * SIDE + j) * chunk, ((2 * a + 1) * SIDE + j) * chunk
            pair = jnp.concatenate(
                [
                    hv[:, :, first : first + chunk].reshape(pairs, chunk),
                    hv[:, :, second : second + chunk].reshape(pairs, chunk),
                ],
                axis=1,
            )
            at = j * slice_w + 2 * a * chunk
            hp[:, at : at + 2 * chunk] = pair

    def pack(q, h):
        je = lax.rem(y + 1 + q, SIDE) * slice_w + h * half_w
        jo = lax.rem(x + 1 + q, SIDE) * slice_w + h * half_w
        je, jo = (pl.ds(pl.multiple_of(j, LANES), half_w) for j in (je, jo))
        hs[q, h, 0:half, :] = _dot(oh[0:half, :], hp[:, je]).astype(BF16)
        hs[q, h, half:rows, :] = _dot(
            oh[half:rows, :], hv[:, :, jo].reshape(pairs, half_w)
        ).astype(BF16)

    def forward_grads(k, d):
        cols = slice(g_cols[k][0], g_cols[k][1] + k * LANES)
        return pltpu.make_async_remote_copy(
            src_ref=gall.at[3 * rows : 4 * rows, cols],
            dst_ref=gall.at[(d - 1) * rows : d * rows, cols],
            send_sem=fg_send.at[k, d - 1],
            recv_sem=fg_recv.at[k, d - 1],
            device_id=gather_peer(d),
            device_id_type=MESH,
        )

    def forward_hidden(q, h):
        return pltpu.make_async_remote_copy(
            src_ref=hin.at[q, h],
            dst_ref=hg.at[q, h],
            send_sem=fh_send.at[q, h],
            recv_sem=fh_recv.at[q, h],
            device_id=gather_peer(q + 1),
            device_id_type=MESH,
        )

    fgs = [[forward_grads(k, d) for d in (1, 2, 3)] for k in range(2)]
    fhs = [[forward_hidden(q, h) for h in range(2)] for q in range(SIDE - 1)]

    def transpose(q, h, rows_in):
        ht[h * half_w : (h + 1) * half_w, q * rows : (q + 1) * rows] = rows_in.T

    def take(q, h):
        fhs[q][h].wait_recv()
        transpose(q, h, hg[q, h])

    n_sq = SIDE * EXPERTS - 1
    sq_copies = []
    for d in (2, 1, 3, 0):
        for i, (dz, dc) in enumerate(zsteps + [(0, 0)]):
            if (d, dz, dc) == (0, 0, 0):
                continue
            pz, pc = z_peer(dz, dc)
            sq_copies.append(
                pltpu.make_async_remote_copy(
                    src_ref=sq_send,
                    dst_ref=sq_recv.at[(d - 1) % SIDE * EXPERTS + i],
                    send_sem=sq_ssem,
                    recv_sem=sq_rsem,
                    device_id=(along(d, pc)[0], pz * 2 + pc),
                    device_id_type=MESH,
                )
            )

    def sq_all(sem):
        return pltpu.make_async_copy(sq_recv.at[0:n_sq], sq_recv.at[0:n_sq], sem)

    takes = {6: [(0, 0)], 7: [(2, 0), (1, 0)], 8: [(0, 1), (2, 1)]}
    for k in range(n_pieces):
        if 1 <= k < n_pieces - 1:
            at = order[k - 1]
            pack(*at)
            for copy in zc[k + 1]:
                copy.start()
            hin[(*at, my_rows)] = hs[(*at, block(z, c))]
        for copy in zc[k]:
            copy.wait_recv()
        if k == 1:
            for copy in id_copies:
                copy.wait_recv()
            ids_in = jnp.concatenate([id_recv[e][:, 0:cap] for e in range(EXPERTS)], axis=1)
            ids_in = jnp.broadcast_to(ids_in, (8, rows)).T[:, 0:1]
            lane = lax.broadcasted_iota(jnp.int32, (rows, LANES), 1).astype(F32) + 1.0
            gall[3 * rows : 4 * rows, out_width:] = jnp.where(ids_in == lane, 1.0, 0.0).astype(BF16)
        if k < 2:
            for copy in fgs[k]:
                copy.start()
            if k == 1:
                g = gall[3 * rows : 4 * rows, 0:out_width]
                b = gall[3 * rows : 4 * rows, out_width:]
                mgram[...] = _dot_t(g, g) * _dot_t(b, b)
        else:
            q, h = order[k - 2]
            if q < SIDE - 1:
                fhs[q][h].start()
            part = hin[q, h]
            gram = _dot_t(part, part)
            if k > 2:
                gram = gram + hgram[...]
            if k + 1 < n_pieces:
                hgram[...] = gram
            else:
                row_sums = jnp.sum(gram * mgram[...], axis=1, keepdims=True)
                member = gall[3 * rows : 4 * rows, out_width:].astype(F32)
                part = jnp.sum(row_sums * member, axis=0, keepdims=True)
                sq_send[...] = part
            if q == SIDE - 1 and h == 0:
                transpose(q, h, hin[q, h])
            for at in takes.get(k, []):
                take(*at)

    for copy in sq_copies:
        copy.start()
    transpose(3, 1, hin[SIDE - 1, 1])
    take(1, 1)
    for copy in fgs[0] + fgs[1]:
        copy.wait_recv()
        copy.wait_send()
    sq_recv[n_sq] = sq_send[...]
    sq_all(sq_rsem).wait()
    norms = jnp.sqrt(jnp.sum(sq_recv[...].reshape(SIDE, EXPERTS, LANES), axis=1))
    norm_out[...] = norms[SIDE - 1 :, 0:EX_BLK] / threshold
    factors = jnp.minimum(1.0, threshold / norms)
    for q in range(SIDE):
        span = slice(q * rows, (q + 1) * rows)
        row_factor = jnp.sum(
            gall[span, out_width:].astype(F32) * factors[q : q + 1, :], axis=1, keepdims=True
        )
        rowf[span, :] = jnp.broadcast_to(row_factor, (rows, LANES))

    def chunk_rows(d, lower, size):
        start = lax.rem(rpos + d, SIDE) * chunk + lower * hc
        return pl.ds(pl.multiple_of(start, 32), size)

    def tile_at(n):
        return pl.ds(pl.multiple_of(n * TILE, TILE), TILE)

    def rs_copy(slot_, n):
        src = (
            part_a.at[n, 0:hc],
            part_b.at[0, n],
            part_c.at[0, n],
            part_a.at[n, hc:chunk],
            part_b.at[1, n],
            part_c.at[1, n],
        )[slot_]
        return pltpu.make_async_remote_copy(
            src_ref=src,
            dst_ref=part_in.at[slot_, n],
            send_sem=rs_send.at[slot_, n],
            recv_sem=rs_recv.at[slot_, n],
            device_id=sum_peer(1 if slot_ < 3 else 3),
            device_id_type=MESH,
        )

    tiles = out_width // TILE

    @pl.loop(0, tiles)
    def _(n):
        cols = tile_at(n)
        wide = jnp.concatenate([rowf[...]] * (TILE // LANES), axis=1)
        gall[:, cols] = (wide * gall[:, cols].astype(F32)).astype(BF16)
        part_a[n] = _dot(ht[chunk_rows(2, 0, chunk), :], gall[:, cols]).astype(BF16)
        rs_copy(0, n).start()
        rs_copy(3, n).start()

    @pl.loop(0, tiles)
    def _(n):
        cols = tile_at(n)
        part_b[0, n] = _dot(ht[chunk_rows(1, 1, hc), :], gall[:, cols]).astype(BF16)
        rs_copy(1, n).start()
        part_b[1, n] = _dot(ht[chunk_rows(3, 0, hc), :], gall[:, cols]).astype(BF16)
        rs_copy(4, n).start()

    @pl.loop(0, tiles)
    def _(n):
        cols = tile_at(n)
        term = _dot(ht[chunk_rows(1, 0, hc), :], gall[:, cols])
        rs_copy(0, n).wait_recv()
        part_c[0, n] = (term + part_in[0, n].astype(F32)).astype(BF16)
        rs_copy(2, n).start()
        term = _dot(ht[chunk_rows(3, 1, hc), :], gall[:, cols])
        rs_copy(3, n).wait_recv()
        part_c[1, n] = (term + part_in[3, n].astype(F32)).astype(BF16)
        rs_copy(5, n).start()

    @pl.loop(0, tiles)
    def _(n):
        cols = tile_at(n)
        own[:, cols] = _dot(ht[chunk_rows(0, 0, chunk), :], gall[:, cols])

    scale = 1.0 / (EX_BLK * SIDE * SIDE)

    @pl.loop(0, tiles)
    def _(n):
        cols = tile_at(n)
        for slot_ in (1, 2, 4, 5):
            rs_copy(slot_, n).wait_recv()
        upper = own[0:hc, cols] + part_in[2, n].astype(F32) + part_in[4, n].astype(F32)
        lower = own[hc:chunk, cols] + part_in[1, n].astype(F32) + part_in[5, n].astype(F32)
        out[0:hc, cols] = (upper * scale).astype(BF16)
        out[hc:chunk, cols] = (lower * scale).astype(BF16)

    for copies in zc + [id_copies]:
        for copy in copies:
            copy.wait_send()
    for copy in fhs[0] + fhs[1] + fhs[2]:
        copy.wait_send()
    sq_all(sq_ssem).wait()

    @pl.loop(0, tiles)
    def _(n):
        for slot_ in range(6):
            rs_copy(slot_, n).wait_send()


def body(hidden, grad_out, gate_weights, routes, example_ids):
    tokens, _, width = hidden.shape
    out_width = grad_out.shape[1]
    rows = 3 * tokens
    slice_w = width // SIDE
    chunk = slice_w // SIDE
    hc = chunk // 2
    wide = out_width + LANES
    tiles = out_width // TILE
    vmem = pl.BlockSpec(memory_space=pltpu.VMEM)
    hbm = pl.BlockSpec(memory_space=pl.ANY)
    dma = pltpu.SemaphoreType.DMA
    update, norms = pl.pallas_call(
        kernel,
        out_shape=(
            pltpu.VMEM((chunk, out_width), BF16),
            pltpu.VMEM((1, EX_BLK), F32),
        ),
        in_specs=[hbm] * 5,
        out_specs=(vmem, vmem),
        scratch_shapes=[
            pltpu.VMEM((2, tokens), jnp.int32),
            pltpu.VMEM((2, tokens), F32),
            pltpu.VMEM((1, tokens), jnp.int32),
            pltpu.VMEM((tokens, 2, width), BF16),
            pltpu.VMEM((2 * tokens, width), BF16),
            pltpu.VMEM((tokens, out_width), BF16),
            pltpu.VMEM((rows, out_width), BF16),
            pltpu.VMEM((SIDE, 2, rows, slice_w // 2), BF16),
            pltpu.VMEM((SIDE * rows, wide), BF16),
            pltpu.VMEM((SIDE, 2, rows, slice_w // 2), BF16),
            pltpu.VMEM((SIDE - 1, 2, rows, slice_w // 2), BF16),
            pltpu.VMEM((slice_w, SIDE * rows), BF16),
            pltpu.VMEM((rows, 2 * tokens), BF16),
            pltpu.VMEM((rows, rows), F32),
            pltpu.VMEM((rows, rows), F32),
            pltpu.VMEM((SIDE * rows, LANES), F32),
            pltpu.VMEM((EXPERTS, 1, LANES), F32),
            pltpu.VMEM((EXPERTS, 1, LANES), F32),
            pltpu.VMEM((1, LANES), F32),
            pltpu.VMEM((SIDE * EXPERTS, 1, LANES), F32),
            pltpu.VMEM((tiles, chunk, TILE), BF16),
            pltpu.VMEM((2, tiles, hc, TILE), BF16),
            pltpu.VMEM((2, tiles, hc, TILE), BF16),
            pltpu.VMEM((6, tiles, hc, TILE), BF16),
            pltpu.VMEM((chunk, out_width), F32),
            dma((5,)),
            dma((2 + 2 * SIDE, EXPERTS - 1)),
            dma((2 + 2 * SIDE, EXPERTS - 1)),
            dma((2, SIDE - 1)),
            dma((2, SIDE - 1)),
            dma((SIDE - 1, 2)),
            dma((SIDE - 1, 2)),
            dma((EXPERTS - 1,)),
            dma((EXPERTS - 1,)),
            dma(()),
            dma(()),
            dma((6, tiles)),
            dma((6, tiles)),
        ],
        compiler_params=pltpu.CompilerParams(
            collective_id=0, has_side_effects=True, vmem_limit_bytes=55 * 1024 * 1024
        ),
    )(routes.T, gate_weights.T, example_ids[None], hidden, grad_out)
    return update[None], norms.reshape(EX_BLK)


def solution(mesh):
    return jax.shard_map(
        body,
        mesh=mesh,
        in_specs=(
            P(("dp", "expert"), None, None),
            P(("dp", "expert"), None),
            P(("dp", "expert"), None),
            P(("dp", "expert"), None),
            P(("dp", "expert")),
        ),
        out_specs=(P("expert", "dp", None), P("dp")),
        check_vma=False,
    )
```

```python
import math

import jax
import jax.numpy as jnp
from jax import lax
from jax.experimental import pallas as pl
from jax.experimental.pallas import tpu as pltpu
from jax.sharding import PartitionSpec as P

MESH = pl.DeviceIdType.MESH
BF16, F32 = jnp.bfloat16, jnp.float32

SIDE = 4
EXPERTS = 8
EX_BLK = 8
LANES = 128
TILE = 256


def _dot(a, b):
    return lax.dot_general(a, b, (((1,), (0,)), ((), ())), preferred_element_type=F32)


def _dot_t(a, b):
    return lax.dot_general(a, b, (((1,), (1,)), ((), ())), preferred_element_type=F32)


def kernel(
    routes_hbm, gates_hbm, ids_hbm, hid, grad, out, norm_out,
    routes, gates, ids,
    hv, hp, gv, gs, hs, gall, hin, hg, ht, oh, hgram, mgram, rowf,
    id_send, id_recv, sq_send, sq_recv, factor_rows, part_a, part_b, part_c, part_in, own,
    in_sem, z_send, z_recv, fg_send, fg_recv, fh_send, fh_recv,
    id_ssem, id_rsem, sq_ssem, sq_rsem, rs_send, rs_recv,
):
    tokens, _, width = hid.shape
    out_width = grad.shape[1]
    cap = 3 * tokens // EXPERTS
    rows = EXPERTS * cap
    half = rows // 2
    slice_w = width // SIDE
    chunk = slice_w // SIDE
    hc = chunk // 2
    g_cols = ((0, out_width // 2), (out_width // 2, out_width))
    half_w = slice_w // 2
    order = [(0, 0), (2, 0), (1, 0), (0, 1), (2, 1), (1, 1), (3, 0), (3, 1)]
    n_pieces = 2 + len(order)
    threshold = math.sqrt(width * out_width * tokens * (0.43 + 0.01 * tokens))

    dp, ex = lax.axis_index("dp"), lax.axis_index("expert")
    x, y = lax.div(dp, SIDE), lax.rem(dp, SIDE)
    z, c = lax.div(ex, 2), lax.rem(ex, 2)
    gpos = y + c * (x - y)
    rpos = x + c * (y - x)

    def along(d, turned):
        a = x * SIDE + lax.rem(y + d, SIDE)
        b = lax.rem(x + d, SIDE) * SIDE + y
        return (a + turned * (b - a), ex)

    def gather_peer(d):
        return along(d, c)

    def sum_peer(d):
        return along(d, 1 - c)

    zsteps = [(2, 0), (2, 1), (1, 0), (3, 0), (1, 1), (3, 1), (0, 1)]

    def z_peer(dz, dc):
        pz = lax.rem(z + dz, SIDE)
        pc = c if dc == 0 else 1 - c
        return pz, pc

    barrier = pltpu.get_barrier_semaphore()
    peers = []
    for dz, dc in zsteps:
        pz, pc = z_peer(dz, dc)
        peers.append((dp, pz * 2 + pc))
    for d in (1, 2, 3):
        peers.append(gather_peer(d))
    for peer in peers:
        pl.semaphore_signal(barrier, inc=1, device_id=peer, device_id_type=MESH)
    small_in = [
        pltpu.make_async_copy(src, dst, in_sem.at[2 + i])
        for i, (src, dst) in enumerate(
            [(routes_hbm, routes), (gates_hbm, gates), (ids_hbm, ids)]
        )
    ]
    g_in = pltpu.make_async_copy(grad, gv, in_sem.at[0])
    h_in = pltpu.make_async_copy(hid, hv, in_sem.at[1])
    for copy in small_in + [g_in, h_in]:
        copy.start()
    for copy in small_in:
        copy.wait()

    pairs = 2 * tokens
    route = jnp.concatenate([routes[0:1, :], routes[1:2, :]], axis=1)
    gate = jnp.concatenate([gates[0:1, :], gates[1:2, :]], axis=1)
    local_id = (ids[0:1, :] - dp * EX_BLK).astype(F32)
    local_id = jnp.concatenate([local_id, local_id], axis=1)
    expert_of = lax.broadcasted_iota(jnp.int32, (EXPERTS, pairs), 0)
    chosen = route == expert_of
    before = lax.broadcasted_iota(jnp.int32, (pairs, pairs), 0) < lax.broadcasted_iota(
        jnp.int32, (pairs, pairs), 1
    )
    place = _dot(
        jnp.where(chosen, 1.0, 0.0).astype(BF16), jnp.where(before, 1.0, 0.0).astype(BF16)
    )
    base = (lax.rem(expert_of, 2) * half + lax.div(expert_of, 2) * cap).astype(F32)
    slot = jnp.sum(jnp.where(chosen, base + place, 0.0), axis=0, keepdims=True)
    hit = slot == lax.broadcasted_iota(jnp.int32, (rows, pairs), 0).astype(F32)
    hot = jnp.where(hit, 1.0, 0.0)
    token_hot = (hot[:, 0:tokens] + hot[:, tokens:]).astype(BF16)
    slot_gate = jnp.sum(jnp.where(hit, gate, 0.0), axis=1, keepdims=True)
    hot16 = hot.astype(BF16)
    slot_id = _dot_t(jnp.broadcast_to(local_id + 1.0, (8, pairs)).astype(BF16), hot16)[0:1, :]
    for j in range(EXPERTS):
        id_send[j] = jnp.concatenate(
            [slot_id[:, j * cap : (j + 1) * cap], jnp.zeros((1, LANES - cap), F32)], axis=1
        )

    def pack_grads(first, last):
        for n in range(first // TILE, last // TILE):
            cols = slice(n * TILE, (n + 1) * TILE)
            gs[:, cols] = (slot_gate * _dot(token_hot, gv[:, cols])).astype(BF16)

    g_in.wait()
    pack_grads(*g_cols[0])
    pl.semaphore_wait(barrier, len(peers))

    my_rows = pl.ds(pl.multiple_of(ex * cap, 16), cap)
    my_grad_rows = pl.ds(pl.multiple_of(3 * rows + ex * cap, 16), cap)

    def block(pz, pc):
        return pl.ds(pl.multiple_of(pc * half + pz * cap, 16), cap)

    def z_copies(k):
        copies = []
        for i, (dz, dc) in enumerate(zsteps):
            pz, pc = z_peer(dz, dc)
            if k < 2:
                cols = slice(*g_cols[k])
                src, dst = gs.at[block(pz, pc), cols], gall.at[my_grad_rows, cols]
            else:
                at = order[k - 2]
                src, dst = hs.at[(*at, block(pz, pc))], hin.at[(*at, my_rows)]
            copies.append(
                pltpu.make_async_remote_copy(
                    src_ref=src,
                    dst_ref=dst,
                    send_sem=z_send.at[k, i],
                    recv_sem=z_recv.at[k, i],
                    device_id=(dp, pz * 2 + pc),
                    device_id_type=MESH,
                )
            )
        return copies

    id_copies = []
    for i, (dz, dc) in enumerate(zsteps):
        pz, pc = z_peer(dz, dc)
        id_copies.append(
            pltpu.make_async_remote_copy(
                src_ref=id_send.at[pc * SIDE + pz],
                dst_ref=id_recv.at[ex],
                send_sem=id_ssem.at[i],
                recv_sem=id_rsem.at[i],
                device_id=(dp, pz * 2 + pc),
                device_id_type=MESH,
            )
        )
    zc = [z_copies(k) for k in range(n_pieces)]
    for copy in zc[0] + id_copies:
        copy.start()

    pack_grads(*g_cols[1])
    for copy in zc[1]:
        copy.start()
    gall[my_grad_rows, 0:out_width] = gs[block(z, c), :]
    id_recv[ex] = id_send[c * SIDE + z]

    from_pair = lax.broadcasted_iota(jnp.int32, (pairs, pairs), 0)
    to_pair = lax.broadcasted_iota(jnp.int32, (pairs, pairs), 1)
    interleave = 2 * lax.rem(from_pair, tokens) + lax.div(from_pair, tokens) == to_pair
    oh[...] = _dot(
        hot16, jnp.where(interleave, 1.0, 0.0).astype(BF16)
    ).astype(BF16)

    h_in.wait()
    for j in range(SIDE):
        for a in range(SIDE // 2):
            first, second = (2 * a * SIDE + j) * chunk, ((2 * a + 1) * SIDE + j) * chunk
            pair = jnp.concatenate(
                [
                    hv[:, :, first : first + chunk].reshape(pairs, chunk),
                    hv[:, :, second : second + chunk].reshape(pairs, chunk),
                ],
                axis=1,
            )
            at = j * slice_w + 2 * a * chunk
            hp[:, at : at + 2 * chunk] = pair

    def pack(q, h):
        je = lax.rem(y + 1 + q, SIDE) * slice_w + h * half_w
        jo = lax.rem(x + 1 + q, SIDE) * slice_w + h * half_w
        je, jo = (pl.ds(pl.multiple_of(j, LANES), half_w) for j in (je, jo))
        hs[q, h, 0:half, :] = _dot(oh[0:half, :], hp[:, je]).astype(BF16)
        hs[q, h, half:rows, :] = _dot(
            oh[half:rows, :], hv[:, :, jo].reshape(pairs, half_w)
        ).astype(BF16)

    def forward_grads(k, d):
        cols = slice(g_cols[k][0], g_cols[k][1] + k * LANES)
        return pltpu.make_async_remote_copy(
            src_ref=gall.at[3 * rows : 4 * rows, cols],
            dst_ref=gall.at[(d - 1) * rows : d * rows, cols],
            send_sem=fg_send.at[k, d - 1],
            recv_sem=fg_recv.at[k, d - 1],
            device_id=gather_peer(d),
            device_id_type=MESH,
        )

    def forward_hidden(q, h):
        return pltpu.make_async_remote_copy(
            src_ref=hin.at[q, h],
            dst_ref=hg.at[q, h],
            send_sem=fh_send.at[q, h],
            recv_sem=fh_recv.at[q, h],
            device_id=gather_peer(q + 1),
            device_id_type=MESH,
        )

    fgs = [[forward_grads(k, d) for d in (1, 2, 3)] for k in range(2)]
    fhs = [[forward_hidden(q, h) for h in range(2)] for q in range(SIDE - 1)]

    def transpose(q, h, rows_in):
        @pl.loop(0, half_w // LANES)
        def _(t):
            at = pl.multiple_of(h * half_w + t * LANES, LANES)
            ht[pl.ds(at, LANES), q * rows : (q + 1) * rows] = rows_in[
                :, pl.ds(pl.multiple_of(t * LANES, LANES), LANES)
            ].T

    def take(q, h):
        fhs[q][h].wait_recv()
        transpose(q, h, hg.at[q, h])

    n_sq = SIDE * EXPERTS - 1
    sq_copies = []
    for d in (2, 1, 3, 0):
        for i, (dz, dc) in enumerate(zsteps + [(0, 0)]):
            if (d, dz, dc) == (0, 0, 0):
                continue
            pz, pc = z_peer(dz, dc)
            sq_copies.append(
                pltpu.make_async_remote_copy(
                    src_ref=sq_send,
                    dst_ref=sq_recv.at[(d - 1) % SIDE * EXPERTS + i],
                    send_sem=sq_ssem,
                    recv_sem=sq_rsem,
                    device_id=(along(d, pc)[0], pz * 2 + pc),
                    device_id_type=MESH,
                )
            )

    def sq_all(sem):
        return pltpu.make_async_copy(sq_recv.at[0:n_sq], sq_recv.at[0:n_sq], sem)

    takes = {6: [(0, 0)], 7: [(2, 0), (1, 0)], 8: [(0, 1), (2, 1)]}
    for k in range(n_pieces):
        if 1 <= k < n_pieces - 1:
            at = order[k - 1]
            pack(*at)
            for copy in zc[k + 1]:
                copy.start()
            hin[(*at, my_rows)] = hs[(*at, block(z, c))]
        for copy in zc[k]:
            copy.wait_recv()
        if k == 1:
            for copy in id_copies:
                copy.wait_recv()
            ids_in = jnp.concatenate([id_recv[e][:, 0:cap] for e in range(EXPERTS)], axis=1)
            ids_in = jnp.broadcast_to(ids_in, (8, rows)).T[:, 0:1]
            lane = lax.broadcasted_iota(jnp.int32, (rows, LANES), 1).astype(F32) + 1.0
            gall[3 * rows : 4 * rows, out_width:] = jnp.where(ids_in == lane, 1.0, 0.0).astype(BF16)
        if k < 2:
            for copy in fgs[k]:
                copy.start()
            if k == 1:
                g = gall[3 * rows : 4 * rows, 0:out_width]
                b = gall[3 * rows : 4 * rows, out_width:]
                mgram[...] = _dot_t(g, g) * _dot_t(b, b)
        else:
            q, h = order[k - 2]
            if q < SIDE - 1:
                fhs[q][h].start()
            part = hin[q, h]
            gram = _dot_t(part, part)
            if k > 2:
                gram = gram + hgram[...]
            if k + 1 < n_pieces:
                hgram[...] = gram
            else:
                row_sums = jnp.sum(gram * mgram[...], axis=1, keepdims=True)
                member = gall[3 * rows : 4 * rows, out_width:].astype(F32)
                part = jnp.sum(row_sums * member, axis=0, keepdims=True)
                sq_send[...] = part
            if q == SIDE - 1 and h == 0:
                transpose(q, h, hin.at[q, h])
            for at in takes.get(k, []):
                take(*at)

    for copy in sq_copies:
        copy.start()
    transpose(3, 1, hin.at[SIDE - 1, 1])
    take(1, 1)
    for copy in fgs[0] + fgs[1]:
        copy.wait_recv()
        copy.wait_send()
    sq_recv[n_sq] = sq_send[...]
    sq_all(sq_rsem).wait()
    norms = jnp.sqrt(jnp.sum(sq_recv[...].reshape(SIDE, EXPERTS, LANES), axis=1))
    norm_out[...] = norms[SIDE - 1 :, 0:EX_BLK] / threshold
    factors = jnp.minimum(1.0, threshold / norms)
    factor_rows[...] = factors

    @pl.loop(0, SIDE)
    def _(q):
        span = pl.ds(pl.multiple_of(q * rows, rows), rows)
        row_factor = jnp.sum(
            gall[span, out_width:].astype(F32) * factor_rows[pl.ds(q, 1), :], axis=1, keepdims=True
        )
        rowf[span, :] = jnp.broadcast_to(row_factor, (rows, LANES))

    def chunk_rows(d, lower, size):
        start = lax.rem(rpos + d, SIDE) * chunk + lower * hc
        return pl.ds(pl.multiple_of(start, 32), size)

    def tile_at(n):
        return pl.ds(pl.multiple_of(n * TILE, TILE), TILE)

    def rs_copy(slot_, n):
        src = (
            part_a.at[n, 0:hc],
            part_b.at[0, n],
            part_c.at[0, n],
            part_a.at[n, hc:chunk],
            part_b.at[1, n],
            part_c.at[1, n],
        )[slot_]
        return pltpu.make_async_remote_copy(
            src_ref=src,
            dst_ref=part_in.at[slot_, n],
            send_sem=rs_send.at[slot_, n],
            recv_sem=rs_recv.at[slot_, n],
            device_id=sum_peer(1 if slot_ < 3 else 3),
            device_id_type=MESH,
        )

    tiles = out_width // TILE

    @pl.loop(0, tiles)
    def _(n):
        cols = tile_at(n)
        wide = jnp.concatenate([rowf[...]] * (TILE // LANES), axis=1)
        gall[:, cols] = (wide * gall[:, cols].astype(F32)).astype(BF16)
        part_a[n] = _dot(ht[chunk_rows(2, 0, chunk), :], gall[:, cols]).astype(BF16)
        rs_copy(0, n).start()
        rs_copy(3, n).start()

    @pl.loop(0, tiles)
    def _(n):
        cols = tile_at(n)
        part_b[0, n] = _dot(ht[chunk_rows(1, 1, hc), :], gall[:, cols]).astype(BF16)
        rs_copy(1, n).start()
        part_b[1, n] = _dot(ht[chunk_rows(3, 0, hc), :], gall[:, cols]).astype(BF16)
        rs_copy(4, n).start()

    @pl.loop(0, tiles)
    def _(n):
        cols = tile_at(n)
        term = _dot(ht[chunk_rows(1, 0, hc), :], gall[:, cols])
        rs_copy(0, n).wait_recv()
        part_c[0, n] = (term + part_in[0, n].astype(F32)).astype(BF16)
        rs_copy(2, n).start()
        term = _dot(ht[chunk_rows(3, 1, hc), :], gall[:, cols])
        rs_copy(3, n).wait_recv()
        part_c[1, n] = (term + part_in[3, n].astype(F32)).astype(BF16)
        rs_copy(5, n).start()

    @pl.loop(0, tiles)
    def _(n):
        cols = tile_at(n)
        own[:, cols] = _dot(ht[chunk_rows(0, 0, chunk), :], gall[:, cols])

    scale = 1.0 / (EX_BLK * SIDE * SIDE)

    @pl.loop(0, tiles)
    def _(n):
        cols = tile_at(n)
        for slot_ in (1, 2, 4, 5):
            rs_copy(slot_, n).wait_recv()
        upper = own[0:hc, cols] + part_in[2, n].astype(F32) + part_in[4, n].astype(F32)
        lower = own[hc:chunk, cols] + part_in[1, n].astype(F32) + part_in[5, n].astype(F32)
        out[0:hc, cols] = (upper * scale).astype(BF16)
        out[hc:chunk, cols] = (lower * scale).astype(BF16)

    for copies in zc + [id_copies]:
        for copy in copies:
            copy.wait_send()
    for copy in fhs[0] + fhs[1] + fhs[2]:
        copy.wait_send()
    sq_all(sq_ssem).wait()

    @pl.loop(0, tiles)
    def _(n):
        for slot_ in range(6):
            rs_copy(slot_, n).wait_send()


def body(hidden, grad_out, gate_weights, routes, example_ids):
    tokens, _, width = hidden.shape
    out_width = grad_out.shape[1]
    rows = 3 * tokens
    slice_w = width // SIDE
    chunk = slice_w // SIDE
    hc = chunk // 2
    wide = out_width + LANES
    tiles = out_width // TILE
    vmem = pl.BlockSpec(memory_space=pltpu.VMEM)
    hbm = pl.BlockSpec(memory_space=pl.ANY)
    dma = pltpu.SemaphoreType.DMA
    update, norms = pl.pallas_call(
        kernel,
        out_shape=(
            pltpu.VMEM((chunk, out_width), BF16),
            pltpu.VMEM((1, EX_BLK), F32),
        ),
        in_specs=[hbm] * 5,
        out_specs=(vmem, vmem),
        scratch_shapes=[
            pltpu.VMEM((2, tokens), jnp.int32),
            pltpu.VMEM((2, tokens), F32),
            pltpu.VMEM((1, tokens), jnp.int32),
            pltpu.VMEM((tokens, 2, width), BF16),
            pltpu.VMEM((2 * tokens, width), BF16),
            pltpu.VMEM((tokens, out_width), BF16),
            pltpu.VMEM((rows, out_width), BF16),
            pltpu.VMEM((SIDE, 2, rows, slice_w // 2), BF16),
            pltpu.VMEM((SIDE * rows, wide), BF16),
            pltpu.VMEM((SIDE, 2, rows, slice_w // 2), BF16),
            pltpu.VMEM((SIDE - 1, 2, rows, slice_w // 2), BF16),
            pltpu.VMEM((slice_w, SIDE * rows), BF16),
            pltpu.VMEM((rows, 2 * tokens), BF16),
            pltpu.VMEM((rows, rows), F32),
            pltpu.VMEM((rows, rows), F32),
            pltpu.VMEM((SIDE * rows, LANES), F32),
            pltpu.VMEM((EXPERTS, 1, LANES), F32),
            pltpu.VMEM((EXPERTS, 1, LANES), F32),
            pltpu.VMEM((1, LANES), F32),
            pltpu.VMEM((SIDE * EXPERTS, 1, LANES), F32),
            pltpu.VMEM((SIDE, LANES), F32),
            pltpu.VMEM((tiles, chunk, TILE), BF16),
            pltpu.VMEM((2, tiles, hc, TILE), BF16),
            pltpu.VMEM((2, tiles, hc, TILE), BF16),
            pltpu.VMEM((6, tiles, hc, TILE), BF16),
            pltpu.VMEM((chunk, out_width), F32),
            dma((5,)),
            dma((2 + 2 * SIDE, EXPERTS - 1)),
            dma((2 + 2 * SIDE, EXPERTS - 1)),
            dma((2, SIDE - 1)),
            dma((2, SIDE - 1)),
            dma((SIDE - 1, 2)),
            dma((SIDE - 1, 2)),
            dma((EXPERTS - 1,)),
            dma((EXPERTS - 1,)),
            dma(()),
            dma(()),
            dma((6, tiles)),
            dma((6, tiles)),
        ],
        compiler_params=pltpu.CompilerParams(
            collective_id=0, has_side_effects=True, vmem_limit_bytes=55 * 1024 * 1024
        ),
    )(routes.T, gate_weights.T, example_ids[None], hidden, grad_out)
    return update[None], norms.reshape(EX_BLK)


def solution(mesh):
    return jax.shard_map(
        body,
        mesh=mesh,
        in_specs=(
            P(("dp", "expert"), None, None),
            P(("dp", "expert"), None),
            P(("dp", "expert"), None),
            P(("dp", "expert"), None),
            P(("dp", "expert")),
        ),
        out_specs=(P("expert", "dp", None), P("dp")),
        check_vma=False,
    )
```

```python
import math

import jax
import jax.numpy as jnp
from jax import lax
from jax.experimental import pallas as pl
from jax.experimental.pallas import tpu as pltpu
from jax.sharding import PartitionSpec as P

MESH = pl.DeviceIdType.MESH
BF16, F32 = jnp.bfloat16, jnp.float32

SIDE = 4
EXPERTS = 8
EX_BLK = 8
LANES = 128
TILE = 256


def _dot(a, b):
    return lax.dot_general(a, b, (((1,), (0,)), ((), ())), preferred_element_type=F32)


def _dot_t(a, b):
    return lax.dot_general(a, b, (((1,), (1,)), ((), ())), preferred_element_type=F32)


def kernel(
    routes_hbm, gates_hbm, ids_hbm, hid, grad, out, norm_out,
    routes, gates, ids,
    hv, hp, gv, gs, hs, gall, hin, hg, ht, oh, hgram, mgram, rowf,
    id_send, id_recv, sq_send, sq_recv, factor_rows, part_a, part_b, part_c, part_in, own,
    in_sem, z_send, z_recv, fg_send, fg_recv, fh_send, fh_recv,
    id_ssem, id_rsem, sq_ssem, sq_rsem, rs_send, rs_recv,
):
    tokens, _, width = hid.shape
    out_width = grad.shape[1]
    cap = 3 * tokens // EXPERTS
    rows = EXPERTS * cap
    half = rows // 2
    slice_w = width // SIDE
    chunk = slice_w // SIDE
    hc = chunk // 2
    g_cols = ((0, out_width // 2), (out_width // 2, out_width))
    half_w = slice_w // 2
    order = [(0, 0), (2, 0), (1, 0), (0, 1), (2, 1), (1, 1), (3, 0), (3, 1)]
    n_pieces = 2 + len(order)
    threshold = math.sqrt(width * out_width * tokens * (0.43 + 0.01 * tokens))

    dp, ex = lax.axis_index("dp"), lax.axis_index("expert")
    x, y = lax.div(dp, SIDE), lax.rem(dp, SIDE)
    z, c = lax.div(ex, 2), lax.rem(ex, 2)
    gpos = y + c * (x - y)
    rpos = x + c * (y - x)

    def along(d, turned):
        a = x * SIDE + lax.rem(y + d, SIDE)
        b = lax.rem(x + d, SIDE) * SIDE + y
        return (a + turned * (b - a), ex)

    def gather_peer(d):
        return along(d, c)

    def sum_peer(d):
        return along(d, 1 - c)

    zsteps = [(2, 0), (2, 1), (1, 0), (3, 0), (1, 1), (3, 1), (0, 1)]

    def z_peer(dz, dc):
        pz = lax.rem(z + dz, SIDE)
        pc = c if dc == 0 else 1 - c
        return pz, pc

    barrier = pltpu.get_barrier_semaphore()
    peers = []
    for dz, dc in zsteps:
        pz, pc = z_peer(dz, dc)
        peers.append((dp, pz * 2 + pc))
    for d in (1, 2, 3):
        peers.append(gather_peer(d))
    for peer in peers:
        pl.semaphore_signal(barrier, inc=1, device_id=peer, device_id_type=MESH)
    small_in = [
        pltpu.make_async_copy(src, dst, in_sem.at[2 + i])
        for i, (src, dst) in enumerate(
            [(routes_hbm, routes), (gates_hbm, gates), (ids_hbm, ids)]
        )
    ]
    g_in = pltpu.make_async_copy(grad, gv, in_sem.at[0])
    h_in = pltpu.make_async_copy(hid, hv, in_sem.at[1])
    for copy in small_in + [g_in, h_in]:
        copy.start()
    for copy in small_in:
        copy.wait()

    pairs = 2 * tokens
    route = jnp.concatenate([routes[0:1, :], routes[1:2, :]], axis=1)
    gate = jnp.concatenate([gates[0:1, :], gates[1:2, :]], axis=1)
    local_id = (ids[0:1, :] - dp * EX_BLK).astype(F32)
    local_id = jnp.concatenate([local_id, local_id], axis=1)
    expert_of = lax.broadcasted_iota(jnp.int32, (EXPERTS, pairs), 0)
    chosen = route == expert_of
    before = lax.broadcasted_iota(jnp.int32, (pairs, pairs), 0) < lax.broadcasted_iota(
        jnp.int32, (pairs, pairs), 1
    )
    place = _dot(
        jnp.where(chosen, 1.0, 0.0).astype(BF16), jnp.where(before, 1.0, 0.0).astype(BF16)
    )
    base = (lax.rem(expert_of, 2) * half + lax.div(expert_of, 2) * cap).astype(F32)
    slot = jnp.sum(jnp.where(chosen, base + place, 0.0), axis=0, keepdims=True)
    hit = slot == lax.broadcasted_iota(jnp.int32, (rows, pairs), 0).astype(F32)
    hot = jnp.where(hit, 1.0, 0.0)
    token_hot = (hot[:, 0:tokens] + hot[:, tokens:]).astype(BF16)
    slot_gate = jnp.sum(jnp.where(hit, gate, 0.0), axis=1, keepdims=True)
    hot16 = hot.astype(BF16)
    slot_id = _dot_t(jnp.broadcast_to(local_id + 1.0, (8, pairs)).astype(BF16), hot16)[0:1, :]
    for j in range(EXPERTS):
        id_send[j] = jnp.concatenate(
            [slot_id[:, j * cap : (j + 1) * cap], jnp.zeros((1, LANES - cap), F32)], axis=1
        )

    def pack_grads(first, last):
        for n in range(first // TILE, last // TILE):
            cols = slice(n * TILE, (n + 1) * TILE)
            gs[:, cols] = (slot_gate * _dot(token_hot, gv[:, cols])).astype(BF16)

    g_in.wait()
    pack_grads(*g_cols[0])
    pl.semaphore_wait(barrier, len(peers))

    my_rows = pl.ds(pl.multiple_of(ex * cap, 16), cap)
    my_grad_rows = pl.ds(pl.multiple_of(3 * rows + ex * cap, 16), cap)

    def block(pz, pc):
        return pl.ds(pl.multiple_of(pc * half + pz * cap, 16), cap)

    def z_copies(k):
        copies = []
        for i, (dz, dc) in enumerate(zsteps):
            pz, pc = z_peer(dz, dc)
            if k < 2:
                cols = slice(*g_cols[k])
                src, dst = gs.at[block(pz, pc), cols], gall.at[my_grad_rows, cols]
            else:
                at = order[k - 2]
                src, dst = hs.at[(*at, block(pz, pc))], hin.at[(*at, my_rows)]
            copies.append(
                pltpu.make_async_remote_copy(
                    src_ref=src,
                    dst_ref=dst,
                    send_sem=z_send.at[k, i],
                    recv_sem=z_recv.at[k, i],
                    device_id=(dp, pz * 2 + pc),
                    device_id_type=MESH,
                )
            )
        return copies

    id_copies = []
    for i, (dz, dc) in enumerate(zsteps):
        pz, pc = z_peer(dz, dc)
        id_copies.append(
            pltpu.make_async_remote_copy(
                src_ref=id_send.at[pc * SIDE + pz],
                dst_ref=id_recv.at[ex],
                send_sem=id_ssem.at[i],
                recv_sem=id_rsem.at[i],
                device_id=(dp, pz * 2 + pc),
                device_id_type=MESH,
            )
        )
    zc = [z_copies(k) for k in range(n_pieces)]
    for copy in zc[0] + id_copies:
        copy.start()

    pack_grads(*g_cols[1])
    for copy in zc[1]:
        copy.start()
    gall[my_grad_rows, 0:out_width] = gs[block(z, c), :]
    id_recv[ex] = id_send[c * SIDE + z]

    from_pair = lax.broadcasted_iota(jnp.int32, (pairs, pairs), 0)
    to_pair = lax.broadcasted_iota(jnp.int32, (pairs, pairs), 1)
    interleave = 2 * lax.rem(from_pair, tokens) + lax.div(from_pair, tokens) == to_pair
    oh[...] = _dot(
        hot16, jnp.where(interleave, 1.0, 0.0).astype(BF16)
    ).astype(BF16)

    h_in.wait()
    for j in range(SIDE):
        for a in range(SIDE // 2):
            first, second = (2 * a * SIDE + j) * chunk, ((2 * a + 1) * SIDE + j) * chunk
            pair = jnp.concatenate(
                [
                    hv[:, :, first : first + chunk].reshape(pairs, chunk),
                    hv[:, :, second : second + chunk].reshape(pairs, chunk),
                ],
                axis=1,
            )
            at = j * slice_w + 2 * a * chunk
            hp[:, at : at + 2 * chunk] = pair

    def pack(q, h):
        je = lax.rem(y + 1 + q, SIDE) * slice_w + h * half_w
        jo = lax.rem(x + 1 + q, SIDE) * slice_w + h * half_w
        je, jo = (pl.ds(pl.multiple_of(j, LANES), half_w) for j in (je, jo))
        hs[q, h, 0:half, :] = _dot(oh[0:half, :], hp[:, je]).astype(BF16)
        hs[q, h, half:rows, :] = _dot(
            oh[half:rows, :], hv[:, :, jo].reshape(pairs, half_w)
        ).astype(BF16)

    def forward_grads(k, d):
        cols = slice(g_cols[k][0], g_cols[k][1] + k * LANES)
        return pltpu.make_async_remote_copy(
            src_ref=gall.at[3 * rows : 4 * rows, cols],
            dst_ref=gall.at[(d - 1) * rows : d * rows, cols],
            send_sem=fg_send.at[k, d - 1],
            recv_sem=fg_recv.at[k, d - 1],
            device_id=gather_peer(d),
            device_id_type=MESH,
        )

    def forward_hidden(q, h):
        return pltpu.make_async_remote_copy(
            src_ref=hin.at[q, h],
            dst_ref=hg.at[q, h],
            send_sem=fh_send.at[q, h],
            recv_sem=fh_recv.at[q, h],
            device_id=gather_peer(q + 1),
            device_id_type=MESH,
        )

    fgs = [[forward_grads(k, d) for d in (1, 2, 3)] for k in range(2)]
    fhs = [[forward_hidden(q, h) for h in range(2)] for q in range(SIDE - 1)]

    def transpose(q, h, rows_in):
        @pl.loop(0, half_w // LANES)
        def _(t):
            at = pl.multiple_of(h * half_w + t * LANES, LANES)
            ht[pl.ds(at, LANES), q * rows : (q + 1) * rows] = rows_in[
                :, pl.ds(pl.multiple_of(t * LANES, LANES), LANES)
            ].T

    def take(q, h):
        fhs[q][h].wait_recv()
        transpose(q, h, hg.at[q, h])

    n_sq = SIDE * EXPERTS - 1
    sq_copies = []
    for d in (2, 1, 3, 0):
        for i, (dz, dc) in enumerate(zsteps + [(0, 0)]):
            if (d, dz, dc) == (0, 0, 0):
                continue
            pz, pc = z_peer(dz, dc)
            sq_copies.append(
                pltpu.make_async_remote_copy(
                    src_ref=sq_send,
                    dst_ref=sq_recv.at[(d - 1) % SIDE * EXPERTS + i],
                    send_sem=sq_ssem,
                    recv_sem=sq_rsem,
                    device_id=(along(d, pc)[0], pz * 2 + pc),
                    device_id_type=MESH,
                )
            )

    def sq_all(sem):
        return pltpu.make_async_copy(sq_recv.at[0:n_sq], sq_recv.at[0:n_sq], sem)

    takes = {6: [(0, 0)], 7: [(2, 0), (1, 0)], 8: [(0, 1), (2, 1)]}
    for k in range(n_pieces):
        if 1 <= k < n_pieces - 1:
            at = order[k - 1]
            pack(*at)
            for copy in zc[k + 1]:
                copy.start()
            hin[(*at, my_rows)] = hs[(*at, block(z, c))]
        for copy in zc[k]:
            copy.wait_recv()
        if k == 1:
            for copy in id_copies:
                copy.wait_recv()
            ids_in = jnp.concatenate([id_recv[e][:, 0:cap] for e in range(EXPERTS)], axis=1)
            ids_in = jnp.broadcast_to(ids_in, (8, rows)).T[:, 0:1]
            lane = lax.broadcasted_iota(jnp.int32, (rows, LANES), 1).astype(F32) + 1.0
            gall[3 * rows : 4 * rows, out_width:] = jnp.where(ids_in == lane, 1.0, 0.0).astype(BF16)
        if k < 2:
            for copy in fgs[k]:
                copy.start()
            if k == 1:
                g = gall[3 * rows : 4 * rows, 0:out_width]
                b = gall[3 * rows : 4 * rows, out_width:]
                mgram[...] = _dot_t(g, g) * _dot_t(b, b)
        else:
            q, h = order[k - 2]
            if q < SIDE - 1:
                fhs[q][h].start()
            part = hin[q, h]
            gram = _dot_t(part, part)
            if k > 2:
                gram = gram + hgram[...]
            if k + 1 < n_pieces:
                hgram[...] = gram
            else:
                row_sums = jnp.sum(gram * mgram[...], axis=1, keepdims=True)
                member = gall[3 * rows : 4 * rows, out_width:].astype(F32)
                part = jnp.sum(row_sums * member, axis=0, keepdims=True)
                sq_send[...] = part
            if q == SIDE - 1 and h == 0:
                transpose(q, h, hin.at[q, h])
            for at in takes.get(k, []):
                take(*at)

    for copy in sq_copies:
        copy.start()
    transpose(3, 1, hin.at[SIDE - 1, 1])
    take(1, 1)
    for copy in fgs[0] + fgs[1]:
        copy.wait_recv()
        copy.wait_send()
    sq_recv[n_sq] = sq_send[...]
    sq_all(sq_rsem).wait()
    norms = jnp.sqrt(jnp.sum(sq_recv[...].reshape(SIDE, EXPERTS, LANES), axis=1))
    norm_out[...] = norms[SIDE - 1 :, 0:EX_BLK] / threshold
    factors = jnp.minimum(1.0, threshold / norms)
    factor_rows[...] = factors

    @pl.loop(0, SIDE)
    def _(q):
        span = pl.ds(pl.multiple_of(q * rows, rows), rows)
        row_factor = jnp.sum(
            gall[span, out_width:].astype(F32) * factor_rows[pl.ds(q, 1), :], axis=1, keepdims=True
        )
        rowf[span, :] = jnp.broadcast_to(row_factor, (rows, LANES))

    def chunk_rows(d, lower, size):
        start = lax.rem(rpos + d, SIDE) * chunk + lower * hc
        return pl.ds(pl.multiple_of(start, 32), size)

    def tile_at(n):
        return pl.ds(pl.multiple_of(n * TILE, TILE), TILE)

    def rs_copy(slot_, n):
        src = (
            part_a.at[n, 0:hc],
            part_b.at[0, n],
            part_c.at[0, n],
            part_a.at[n, hc:chunk],
            part_b.at[1, n],
            part_c.at[1, n],
        )[slot_]
        return pltpu.make_async_remote_copy(
            src_ref=src,
            dst_ref=part_in.at[slot_, n],
            send_sem=rs_send.at[slot_, n],
            recv_sem=rs_recv.at[slot_, n],
            device_id=sum_peer(1 if slot_ < 3 else 3),
            device_id_type=MESH,
        )

    tiles = out_width // TILE

    @pl.loop(0, tiles)
    def _(n):
        cols = tile_at(n)
        wide = jnp.concatenate([rowf[...]] * (TILE // LANES), axis=1)
        gall[:, cols] = (wide * gall[:, cols].astype(F32)).astype(BF16)
        part_a[n, 0:hc] = _dot(ht[chunk_rows(2, 0, hc), :], gall[:, cols]).astype(BF16)
        rs_copy(0, n).start()
        part_a[n, hc:chunk] = _dot(ht[chunk_rows(2, 1, hc), :], gall[:, cols]).astype(BF16)
        rs_copy(3, n).start()

    @pl.loop(0, tiles)
    def _(n):
        cols = tile_at(n)
        part_b[0, n] = _dot(ht[chunk_rows(1, 1, hc), :], gall[:, cols]).astype(BF16)
        rs_copy(1, n).start()
        part_b[1, n] = _dot(ht[chunk_rows(3, 0, hc), :], gall[:, cols]).astype(BF16)
        rs_copy(4, n).start()

    @pl.loop(0, tiles)
    def _(n):
        cols = tile_at(n)
        term = _dot(ht[chunk_rows(1, 0, hc), :], gall[:, cols])
        rs_copy(0, n).wait_recv()
        part_c[0, n] = (term + part_in[0, n].astype(F32)).astype(BF16)
        rs_copy(2, n).start()
        term = _dot(ht[chunk_rows(3, 1, hc), :], gall[:, cols])
        rs_copy(3, n).wait_recv()
        part_c[1, n] = (term + part_in[3, n].astype(F32)).astype(BF16)
        rs_copy(5, n).start()

    @pl.loop(0, tiles)
    def _(n):
        cols = tile_at(n)
        own[:, cols] = _dot(ht[chunk_rows(0, 0, chunk), :], gall[:, cols])

    scale = 1.0 / (EX_BLK * SIDE * SIDE)

    @pl.loop(0, tiles)
    def _(n):
        cols = tile_at(n)
        for slot_ in (1, 2, 4, 5):
            rs_copy(slot_, n).wait_recv()
        upper = own[0:hc, cols] + part_in[2, n].astype(F32) + part_in[4, n].astype(F32)
        lower = own[hc:chunk, cols] + part_in[1, n].astype(F32) + part_in[5, n].astype(F32)
        out[0:hc, cols] = (upper * scale).astype(BF16)
        out[hc:chunk, cols] = (lower * scale).astype(BF16)

    for copies in zc + [id_copies]:
        for copy in copies:
            copy.wait_send()
    for copy in fhs[0] + fhs[1] + fhs[2]:
        copy.wait_send()
    sq_all(sq_ssem).wait()

    @pl.loop(0, tiles)
    def _(n):
        for slot_ in range(6):
            rs_copy(slot_, n).wait_send()


def body(hidden, grad_out, gate_weights, routes, example_ids):
    tokens, _, width = hidden.shape
    out_width = grad_out.shape[1]
    rows = 3 * tokens
    slice_w = width // SIDE
    chunk = slice_w // SIDE
    hc = chunk // 2
    wide = out_width + LANES
    tiles = out_width // TILE
    vmem = pl.BlockSpec(memory_space=pltpu.VMEM)
    hbm = pl.BlockSpec(memory_space=pl.ANY)
    dma = pltpu.SemaphoreType.DMA
    update, norms = pl.pallas_call(
        kernel,
        out_shape=(
            pltpu.VMEM((chunk, out_width), BF16),
            pltpu.VMEM((1, EX_BLK), F32),
        ),
        in_specs=[hbm] * 5,
        out_specs=(vmem, vmem),
        scratch_shapes=[
            pltpu.VMEM((2, tokens), jnp.int32),
            pltpu.VMEM((2, tokens), F32),
            pltpu.VMEM((1, tokens), jnp.int32),
            pltpu.VMEM((tokens, 2, width), BF16),
            pltpu.VMEM((2 * tokens, width), BF16),
            pltpu.VMEM((tokens, out_width), BF16),
            pltpu.VMEM((rows, out_width), BF16),
            pltpu.VMEM((SIDE, 2, rows, slice_w // 2), BF16),
            pltpu.VMEM((SIDE * rows, wide), BF16),
            pltpu.VMEM((SIDE, 2, rows, slice_w // 2), BF16),
            pltpu.VMEM((SIDE - 1, 2, rows, slice_w // 2), BF16),
            pltpu.VMEM((slice_w, SIDE * rows), BF16),
            pltpu.VMEM((rows, 2 * tokens), BF16),
            pltpu.VMEM((rows, rows), F32),
            pltpu.VMEM((rows, rows), F32),
            pltpu.VMEM((SIDE * rows, LANES), F32),
            pltpu.VMEM((EXPERTS, 1, LANES), F32),
            pltpu.VMEM((EXPERTS, 1, LANES), F32),
            pltpu.VMEM((1, LANES), F32),
            pltpu.VMEM((SIDE * EXPERTS, 1, LANES), F32),
            pltpu.VMEM((SIDE, LANES), F32),
            pltpu.VMEM((tiles, chunk, TILE), BF16),
            pltpu.VMEM((2, tiles, hc, TILE), BF16),
            pltpu.VMEM((2, tiles, hc, TILE), BF16),
            pltpu.VMEM((6, tiles, hc, TILE), BF16),
            pltpu.VMEM((chunk, out_width), F32),
            dma((5,)),
            dma((2 + 2 * SIDE, EXPERTS - 1)),
            dma((2 + 2 * SIDE, EXPERTS - 1)),
            dma((2, SIDE - 1)),
            dma((2, SIDE - 1)),
            dma((SIDE - 1, 2)),
            dma((SIDE - 1, 2)),
            dma((EXPERTS - 1,)),
            dma((EXPERTS - 1,)),
            dma(()),
            dma(()),
            dma((6, tiles)),
            dma((6, tiles)),
        ],
        compiler_params=pltpu.CompilerParams(
            collective_id=0, has_side_effects=True, vmem_limit_bytes=55 * 1024 * 1024
        ),
    )(routes.T, gate_weights.T, example_ids[None], hidden, grad_out)
    return update[None], norms.reshape(EX_BLK)


def solution(mesh):
    return jax.shard_map(
        body,
        mesh=mesh,
        in_specs=(
            P(("dp", "expert"), None, None),
            P(("dp", "expert"), None),
            P(("dp", "expert"), None),
            P(("dp", "expert"), None),
            P(("dp", "expert")),
        ),
        out_specs=(P("expert", "dp", None), P("dp")),
        check_vma=False,
    )
```
